32 devices in a mesh: row: 4 (over x, core), col: 8 (over z, y).
Axes of the slice: x: 2, y: 2, z: 4, core: 2. Of those that a mesh axis runs over, the one named last changes fastest.
Arguments:
- vectors: float32 [16, 8, 64, 256], P(None, 'row', 'col'), may hold values from -6 to 6
- leaf_order: int32 [8, 64, 256], P('row', 'col'), may hold values from 0 to 255, each once within a row
- offsets: float32 [3, 8, 64, 256], P(None, 'row', 'col'), may hold values from 0 to 1
- near_mask: int32 [9, 8, 64], P(None, 'row', 'col'), may hold values 0 or 1
- far_mask: int32 [16, 8, 64], P(None, 'row', 'col'), may hold values 0 or 1
- basis: float32 [8, 64, 64, 256], P('row', 'col'), may hold values from -0.375 to 0.375
- transfer: float32 [8, 64, 64, 64], P('row', 'col'), may hold values from -0.75 to 0.75
- coupling: float32 [16, 64, 64], replicated, may hold values from -0.25 to 0.25
- top_coupling: float32 [16, 64, 64], replicated, may hold values from -0.03125 to 0.03125
- cluster_owner: int32 [4, 8], P('row', 'col'), may hold values from 0 to 15
Outputs:
- product: float32 [16, 8, 64, 256], P(None, 'row', 'col')
The draws below stay inside these ranges and needn't reach their ends.
Inputs may be any that keep to these rules, and one draw needn't show every extreme that they name: `leaf_order`: each leaf's entries are a permutation of 0 to 255.
All inputs are finite; a program needn't handle non-finite values. No bound on the sum of `near_mask` or of `far_mask` on one device may be relied on, other than what follows from the above.
Results may differ from the reference program's by a relative error of at most 0.0003.
Values sent between devices are 32-bit elements; how exact they have to be, the bound alone decides.
No kernel may reach another device: no remote copies, remote signals or barrier semaphores. Data moves between devices by JAX's collectives and lax.ppermute only.
A program may use at most 64 MiB of HBM per device.

```python
import math
import jax
import jax.numpy as jnp
from jax import lax

LEAF = 256
RANK = 64
RHS = 16
LR = 2
LC = 8
TOPN = 16
LEAFR = 8
LEAFC = 64
N_ROW = 4
N_COL = 8


def with_ends(drawn, stream_key, least, high):
    shape = drawn.shape
    spot = [jax.random.randint(jax.random.fold_in(stream_key, axis), (), 0, shape[axis]) for axis in range(len(shape))]
    drawn = drawn.at[tuple(spot)].set(least)
    longest = shape.index(max(shape))
    spot[longest] = (spot[longest] + 1) % shape[longest]
    return drawn.at[tuple(spot)].set(high)


def block_scale(stream_key, dims, cuts, least, high):
    factor_of = 1.0
    for axis_at, parts in cuts:
        draws = jax.random.uniform(jax.random.fold_in(jax.random.fold_in(stream_key, 6), axis_at), (parts,), jnp.float32, least / len(cuts), high / len(cuts))
        factor_of = factor_of * jnp.repeat(jnp.exp(draws), dims[axis_at] // parts).reshape((-1,) + (1,) * (len(dims) - 1 - axis_at))
    return factor_of


def noise(stream_key, shape, width, most, cuts=(), kind=jnp.bfloat16):
    values = width * jax.random.normal(stream_key, shape, jnp.float32)
    if cuts:
        values = values * block_scale(stream_key, shape, cuts, -0.22, 0.18)
    return jnp.clip(values, -most, most).astype(kind)


def setup_inputs(seed: int = 0) -> dict:
    key_of = jax.random.split(jax.random.key(seed), 11)
    vectors = noise(key_of[0], (RHS, LEAFR, LEAFC, LEAF), 1.0, 6.0, ((1, 4), (2, 8)), jnp.float32)
    leaf_order = jax.vmap(lambda own: jax.random.permutation(own, LEAF))(jax.random.split(key_of[1], LEAFR * LEAFC)).reshape((LEAFR, LEAFC, LEAF)).astype(jnp.int32)
    offsets = jnp.clip(1.0 * jax.random.uniform(key_of[2], (3, LEAFR, LEAFC, LEAF), jnp.float32) ** block_scale(key_of[2], (3, LEAFR, LEAFC, LEAF), ((1, 4), (2, 8)), -0.2, 0.2), 0.0, 1.0)
    near_mask = with_ends((jax.random.randint(key_of[3], (9, LEAFR, LEAFC), 0, 4) < 3).astype(jnp.int32), jax.random.fold_in(key_of[3], 1), 0, 1)
    far_mask = with_ends((jax.random.randint(key_of[4], (16, LEAFR, LEAFC), 0, 2) < 1).astype(jnp.int32), jax.random.fold_in(key_of[4], 1), 0, 1)
    basis = noise(key_of[5], (LEAFR, LEAFC, RANK, LEAF), LEAF ** -0.5, 0.375, ((0, 4), (1, 8)), jnp.float32)
    transfer = noise(key_of[6], (LEAFR, LEAFC, RANK, RANK), RANK ** -0.5, 0.75, ((0, 4), (1, 8)), jnp.float32)
    coupling = noise(key_of[7], (16, RANK, RANK), (RANK * 8) ** -0.5, 0.25, (), jnp.float32)
    top_coupling = noise(key_of[8], (TOPN, RANK, RANK), (RANK * LR * LC * N_ROW * N_COL) ** -0.5, 0.03125, (), jnp.float32)
    cluster_owner = with_ends(jax.random.randint(key_of[9], (N_ROW, N_COL), 0, TOPN), jax.random.fold_in(key_of[9], 1), 0, TOPN - 1).astype(jnp.int32)
    return dict(vectors=vectors, leaf_order=leaf_order, offsets=offsets, near_mask=near_mask, far_mask=far_mask, basis=basis, transfer=transfer, coupling=coupling, top_coupling=top_coupling, cluster_owner=cluster_owner)


softening = 0.01

def far_offsets():
    found = []
    for down_step in range(-2, 3):
        for right_step in range(-2, 3):
            if max(abs(down_step), abs(right_step)) == 2:
                found.append((down_step, right_step))
    return found

def kernel_block(target, source):
    square = jnp.zeros(target.shape[1:] + (source.shape[-1],), jnp.float32)
    for comp in range(3):
        diff = target[comp][..., :, None] - source[comp][..., None, :]
        square = square + diff * diff
    return 1.0 / jnp.sqrt(square + softening)

def near_term(target, source, values, weight):
    tile = kernel_block(target, source) * weight.astype(jnp.float32)[:, :, None, None]
    return jnp.einsum('abij,sabj->sabi', tile, values, precision=lax.Precision.HIGHEST)

def inverse_order(order):
    flat = order.reshape(-1, order.shape[-1])
    iota = jnp.broadcast_to(jnp.arange(flat.shape[1], dtype=jnp.int32)[None, :], flat.shape)
    lines = jnp.broadcast_to(jnp.arange(flat.shape[0], dtype=jnp.int32)[:, None], flat.shape)
    inverse = jnp.zeros_like(flat).at[lines, flat].set(iota)
    return inverse.reshape(order.shape)

def reference(vectors, leaf_order, offsets, near_mask, far_mask, basis, transfer, coupling, top_coupling, cluster_owner):
    hp = lax.Precision.HIGHEST
    sorted_vec = jnp.take_along_axis(vectors, leaf_order[None], axis=3)
    row_pos = jnp.arange(LEAFR, dtype=jnp.float32)[:, None, None] + offsets[0]
    col_pos = jnp.arange(LEAFC, dtype=jnp.float32)[None, :, None] + offsets[1]
    pos = jnp.stack([row_pos, col_pos, 0.25 * offsets[2]], 0)
    pad_spec = ((0, 0), (1, 1), (1, 1), (0, 0))
    pos_pad = jnp.pad(pos, pad_spec)
    vec_pad = jnp.pad(sorted_vec, pad_spec)

    def near_row(line):
        target = lax.dynamic_slice_in_dim(pos, line, 1, 1)
        total = jnp.zeros((RHS, 1, LEAFC, LEAF), jnp.float32)
        for down_step in (-1, 0, 1):
            for right_step in (-1, 0, 1):
                slot = 3 * (down_step + 1) + right_step + 1
                source = lax.dynamic_slice_in_dim(pos_pad, line + 1 + down_step, 1, 1)[:, :, 1 + right_step:1 + right_step + LEAFC]
                values = lax.dynamic_slice_in_dim(vec_pad, line + 1 + down_step, 1, 1)[:, :, 1 + right_step:1 + right_step + LEAFC]
                weight = lax.dynamic_slice_in_dim(near_mask[slot], line, 1, 0)
                total = total + near_term(target, source, values, weight)
        return total[:, 0]
    lines_out = lax.map(near_row, jnp.arange(LEAFR, dtype=jnp.int32))
    near = jnp.transpose(lines_out, (1, 0, 2, 3)) * (1.0 / (3.0 * math.sqrt(LEAF)))
    coef = jnp.einsum('abkp,sabp->ksab', basis, sorted_vec, precision=hp)
    coef_pad = jnp.pad(coef, ((0, 0), (0, 0), (2, 2), (2, 2)))
    far = jnp.zeros_like(coef)
    for slot, (down_step, right_step) in enumerate(far_offsets()):
        window = coef_pad[:, :, 2 + down_step:2 + down_step + LEAFR, 2 + right_step:2 + right_step + LEAFC]
        moved = jnp.einsum('jk,ksab->jsab', coupling[slot], window, precision=hp)
        far = far + moved * far_mask[slot].astype(jnp.float32)[None, None]
    shaped_transfer = transfer.reshape(N_ROW, LR, N_COL, LC, RANK, RANK)
    shaped_coef = coef.reshape(RANK, RHS, N_ROW, LR, N_COL, LC)
    cluster = jnp.einsum('xaybkj,ksxayb->xyjs', shaped_transfer, shaped_coef, precision=hp)
    nodes = jnp.arange(TOPN, dtype=jnp.int32)
    onehot = (cluster_owner[None] == nodes[:, None, None]).astype(jnp.float32)
    top = jnp.einsum('gxy,xyjs->gjs', onehot, cluster, precision=hp)
    table = top_coupling[(nodes[:, None] - nodes[None, :]) % TOPN]
    keep = (nodes[:, None] != nodes[None, :]).astype(jnp.float32)
    top_local = jnp.einsum('gh,ghjk,hks->gjs', keep, table, top, precision=hp)
    device_local = jnp.einsum('gxy,gjs->xyjs', onehot, top_local, precision=hp)
    down = jnp.einsum('xaybkj,xyjs->ksxayb', shaped_transfer, device_local, precision=hp)
    local = far + down.reshape(RANK, RHS, LEAFR, LEAFC)
    result = near + jnp.einsum('abkp,ksab->sabp', basis, local, precision=hp)
    return jnp.take_along_axis(result, inverse_order(leaf_order)[None], axis=3)
```

```python
import functools

import jax
import jax.numpy as jnp
import numpy as np
from jax import lax
from jax.experimental import pallas as pl
from jax.experimental.pallas import tpu as pltpu
from jax.sharding import PartitionSpec as P

softening = 0.01
F32 = jnp.float32
BF16 = jnp.bfloat16
AXES = ("row", "col")
NT = (((1,), (1,)), ((), ()))
TN = (((0,), (0,)), ((), ()))
NN = (((1,), (0,)), ((), ()))
FEATS = 16
K = 32


def far_offsets():
    found = []
    for down_step in range(-2, 3):
        for right_step in range(-2, 3):
            if max(abs(down_step), abs(right_step)) == 2:
                found.append((down_step, right_step))
    return found


def dot(a, b, dims=NN):
    return lax.dot_general(a, b, dims, preferred_element_type=F32)


def split(x):
    hi = x.astype(BF16)
    lo = (x - hi.astype(F32)).astype(BF16)
    return hi, lo


def dot3(a, b, dims=NN):
    ah, al = split(a)
    bh, bl = split(b)
    return dot(ah, bh, dims) + dot(al, bh, dims) + dot(ah, bl, dims)


def strided(ref, start, half, count, stride):
    first = ref[pl.ds(start, count, stride=stride), :]
    second = ref[pl.ds(start + half, count, stride=stride), :]
    return jnp.concatenate([first, second], 1)


def put_strided(ref, start, half, count, stride, x):
    ref[pl.ds(start, count, stride=stride), :] = x[:, :128]
    ref[pl.ds(start + half, count, stride=stride), :] = x[:, 128:]


def products(slot):
    step = (slot // 3 - 1, slot % 3 - 1)
    one = 9
    found = []
    for comp in range(3):
        for mine in range(2):
            for other in range(2):
                found.append((2 * comp + mine, 2 * comp + other, -2.0))
    for part in range(3):
        found.append((6 + part, one, 1.0))
        found.append((one, 6 + part, 1.0))
    for comp in range(2):
        for part in range(2):
            found.append((2 * comp + part, one, 2.0 * step[comp]))
            found.append((one, 2 * comp + part, -2.0 * step[comp]))
    rest = np.float32(softening)
    for _ in range(3):
        part = np.float32(np.asarray(rest, jnp.bfloat16))
        found.append((one, one, float(part)))
        rest = np.float32(rest - part)
    found.append((one, one, float(step[0] ** 2 + step[1] ** 2)))
    return found


def source_choice():
    feat = lax.broadcasted_iota(jnp.int32, (FEATS, K), 0)
    at = lax.broadcasted_iota(jnp.int32, (FEATS, K), 1)
    chosen = jnp.zeros((FEATS, K), F32)
    for i, (mine, _, _) in enumerate(products(0)):
        chosen = jnp.where((at == i) & (feat == mine), 1.0, chosen)
    return chosen.astype(BF16)


def target_choice():
    at = lax.broadcasted_iota(jnp.int32, (K, FEATS), 0)
    feat = lax.broadcasted_iota(jnp.int32, (K, FEATS), 1)
    chosen = jnp.zeros((K, FEATS), F32)
    for i, (_, other, _) in enumerate(products(0)):
        chosen = jnp.where((at == i) & (feat == other), 1.0, chosen)
    return chosen.astype(BF16)


def put_factors(factors):
    at = lax.broadcasted_iota(jnp.int32, (K, 128), 0)
    for slot in range(9):
        factor = jnp.zeros((K, 128), F32)
        for i, (_, _, value) in enumerate(products(slot)):
            if value:
                factor = jnp.where(at == i, value, factor)
        factors[slot] = factor.astype(BF16)


def start_all(pairs, sems):
    copies = [pltpu.make_async_copy(src, dst, sems.at[i]) for i, (src, dst) in enumerate(pairs)]
    for copy in copies:
        copy.start()
    return copies


def prepare_kernel(rows, cols, rhs, rank, leaf, nodes,
                   owner_ref, vec_any, order_any, off_any, basis_any, transfer_any, table_any,
                   pos_ref, coef_ref, basis_out, sent_ref, owner_out,
                   vec, order, off, basis, transfer, table, feat, rolled, sems):
    leaves = rows * cols
    lines = 2 * leaves
    copies = start_all(
        [(order_any, order), (off_any, off), (basis_any, basis), (vec_any, vec), (transfer_any, transfer), (table_any, table)],
        sems,
    )
    copies[0].wait()
    copies[1].wait()
    for comp in range(3):
        u = off[pl.ds(comp * lines, lines), :] - 0.5
        if comp == 2:
            u = u * 0.25
        hi = u.astype(BF16).astype(F32)
        feat[pl.ds(2 * comp * lines, lines), :] = hi
        feat[pl.ds((2 * comp + 1) * lines, lines), :] = (u - hi).astype(BF16).astype(F32)
    feat[pl.ds(6 * lines, 10 * lines), :] = jnp.zeros((10 * lines, 128), F32)
    copies[2].wait()
    copies[3].wait()
    spots = lax.broadcasted_iota(jnp.int32, (leaf, leaf), 0)
    coefs = []
    for at in range(leaves):
        start = (at // cols) * 2 * cols + at % cols
        own_order = jnp.concatenate([order[pl.ds(start, 1), :], order[pl.ds(start + cols, 1), :]], 1)
        chosen = (jnp.broadcast_to(own_order, (leaf, leaf)) == spots).astype(F32).astype(BF16)
        bh, bl = split(basis[at])
        own = strided(feat, start, cols, FEATS, lines).astype(BF16)
        moved = dot(jnp.concatenate([bh, bl, own], 0), chosen, NT)
        both = moved[: 2 * rank].astype(BF16)
        basis_out[at] = both
        offs = moved[2 * rank :]
        for comp in range(3):
            line = offs[2 * comp : 2 * comp + 1] + offs[2 * comp + 1 : 2 * comp + 2]
            pos_ref[pl.ds(comp * lines + start, 1), :] = line[:, :128]
            pos_ref[pl.ds(comp * lines + start + cols, 1), :] = line[:, 128:]
        xh, xl = split(strided(vec, start, cols, rhs, lines))
        four = dot(jnp.concatenate([xh, xl], 0), both, NT)
        coefs.append(four[:rhs, :rank] + four[:rhs, rank:] + four[rhs:, :rank] + four[rhs:, rank:])
    wide = [jnp.concatenate([coefs[2 * p], coefs[2 * p + 1]], 1) for p in range(leaves // 2)]
    row = jnp.where(lax.rem(lax.axis_index("row"), 2) == 0, 0, (rows - 1) * 2 * cols)
    for comp in range(3 + rhs):
        ref, first = (pos_ref, comp) if comp < 3 else (vec, comp - 3)
        sent_ref[pl.ds(comp * 2 * cols, 2 * cols), :] = ref[pl.ds(pl.multiple_of(first * lines + row, 2 * cols), 2 * cols), :]
    near_rows = (3 + rhs) * 2 * cols
    for p in range(leaves // 2):
        coef_ref[pl.ds(p * rhs, rhs), :] = wide[p]
        sent_ref[pl.ds(near_rows + p * rhs, rhs), :] = wide[p]
    copies[4].wait()
    cluster = dot3(jnp.concatenate(wide, 1), transfer[...])
    copies[5].wait()
    owner = owner_ref[0, 0]
    owner_out[...] = jnp.full(owner_out.shape, owner, jnp.int32)
    for node in range(nodes):
        gap = lax.rem(node - owner + nodes, nodes)
        rolled[pl.ds(node * rank, rank), :] = table[gap] * jnp.where(gap == 0, 0.0, 1.0)
    terms = dot3(cluster, rolled[...], NT)
    for pair in range(nodes // 2):
        sent_ref[pl.ds(near_rows + leaves // 2 * rhs + pair * rhs, rhs), :] = terms[:, pair * 2 * rank : (pair + 1) * 2 * rank]


def fill(into, ref, lines):
    total = jnp.zeros((lines, 128), F32)
    for comp in range(3):
        u = ref[pl.ds(comp * lines, lines), :]
        hi = u.astype(BF16).astype(F32)
        into[pl.ds(2 * comp * lines, lines), :] = hi
        into[pl.ds((2 * comp + 1) * lines, lines), :] = u - hi
        total = total + u * u
    for part in range(3):
        hi = total.astype(BF16).astype(F32)
        into[pl.ds((6 + part) * lines, lines), :] = hi
        total = total - hi
    into[pl.ds(9 * lines, lines), :] = jnp.ones((lines, 128), F32)
    into[pl.ds(10 * lines, 6 * lines), :] = jnp.zeros((6 * lines, 128), F32)


def step_target(targets, factors, at, slot):
    factor = factors[slot]
    return targets[at] * jnp.concatenate([factor, factor], 1)


def place(points, feats, spread, values, source_map, rhs, start, half, stride, at):
    own = strided(feats, start, half, FEATS, stride).astype(BF16)
    spread[at] = dot(own, source_map, TN).astype(BF16)
    xh, xl = split(strided(points, 3 * stride + start, half, rhs, stride))
    values[at] = jnp.concatenate([xh, xl], 0)


def tile_product(spread, target, values, keep):
    kh, kl = split(lax.rsqrt(dot(spread, target)))
    x = jnp.where(keep, values, jnp.zeros_like(values))
    rhs = x.shape[0] // 2
    first = dot(x, kh)
    return first[:rhs] + first[rhs:] + dot(x[:rhs], kl)


def own_kernel(rows, cols, rhs, rank, leaf,
               mask_any, vec, pos_ref,
               near_ref, targets, factors,
               near_mask, feat, spread, values, sems):
    copies = start_all([(mask_any, near_mask)], sems)
    leaves = rows * cols
    lines = 2 * leaves
    fill(feat, pos_ref, lines)
    put_factors(factors)
    source_map, target_map = source_choice(), target_choice()
    for at in range(leaves):
        start = (at // cols) * 2 * cols + at % cols
        own = strided(feat, start, cols, FEATS, lines).astype(BF16)
        spread[at] = dot(own, source_map, TN).astype(BF16)
        targets[at] = dot(target_map, own).astype(BF16)
        xh, xl = split(strided(vec, start, cols, rhs, lines))
        values[at] = jnp.concatenate([xh, xl], 0)
    copies[0].wait()
    for at in range(leaves):
        row, col = at // cols, at % cols
        total = jnp.zeros((rhs, leaf), F32)
        for slot in range(9):
            to_row, to_col = row + slot // 3 - 1, col + slot % 3 - 1
            if 0 <= to_row < rows and 0 <= to_col < cols:
                other = to_row * cols + to_col
                total = total + tile_product(
                    spread[other], step_target(targets, factors, at, slot), values[other], near_mask[row, col, slot] != 0
                )
        near_ref[at] = total


def down_kernel(leaves, rank, basis_ref, transfer, down_ref):
    for at in range(leaves):
        both = basis_ref[at]
        th, tl = split(transfer[pl.ds(at * rank, rank), :])
        moved = dot(th, both[:rank], TN) + dot(tl, both[:rank], TN) + dot(th, both[rank:], TN)
        gh, gl = split(moved)
        down_ref[at] = jnp.concatenate([gh, gl], 0)


def gather_kernel(rows, cols, rhs, n_row, merged,
                  vec_any, vec_sib_any, pos_sib_any, coef_sib_any, got_any, pos, coef, sent_ref,
                  above_ref, below_ref, coef_ref, even_ref, odd_ref,
                  vec, vec_sib, pos_sib, coef_sib, got, sems):
    copies = start_all(
        [(vec_any, vec), (vec_sib_any, vec_sib), (pos_sib_any, pos_sib), (coef_sib_any, coef_sib), (got_any, got)], sems
    )
    comps = 3 + rhs
    lines = 2 * rows * cols
    line = 2 * cols
    my_row = lax.axis_index("row")
    row_even = lax.rem(my_row, 2) == 0
    col_even = lax.rem(lax.axis_index("col"), 2) == 0
    beyond = jnp.where(row_even, my_row > 0, my_row < n_row - 1)
    for copy in copies:
        copy.wait()
    row = jnp.where(row_even, 0, (rows - 1) * line)
    for comp in range(comps):
        ref, first = (pos_sib, comp) if comp < 3 else (vec_sib, comp - 3)
        near = ref[pl.ds(pl.multiple_of(first * lines + row, line), line), :]
        mine = pl.ds(comp * line, line)
        far = jnp.where(beyond, got[mine, :], 0.0)
        above_ref[mine, :] = jnp.where(row_even, far, near)
        below_ref[mine, :] = jnp.where(row_even, near, far)
    block = coef.shape[0]
    near = coef_sib[...]
    far = jnp.where(beyond, got[pl.ds(comps * line, block), :], 0.0)
    coef_ref[pl.ds(0, block), :] = jnp.where(row_even, far, near)
    coef_ref[pl.ds(block, block), :] = coef[...]
    coef_ref[pl.ds(2 * block, block), :] = jnp.where(row_even, near, far)

    def send(low, high, start, count, stride):
        where = pl.ds(start, count) if stride == 1 else pl.ds(start, count, stride=stride)
        even_ref[where, :] = jnp.where(col_even, high, low)
        odd_ref[where, :] = jnp.where(col_even, low, high)

    def column(ref, start, count, stride):
        return [ref[pl.ds(start + at, count, stride=stride), :] for at in (0, cols - 1)]

    side = 2 * (rows + 2)
    for half in range(2):
        send(*column(above_ref, half * cols, comps, line), half, comps, side)
        send(*column(below_ref, half * cols, comps, line), 2 * (rows + 1) + half, comps, side)
        for r in range(rows):
            to = 2 * (r + 1) + half
            send(*column(pos, (2 * r + half) * cols, 3, lines), to, 3, side)
            send(*column(vec, (2 * r + half) * cols, rhs, lines), 3 * side + to, rhs, side)
    pairs = cols // 2
    for at in range(3 * rows):
        low = coef_ref[pl.ds(at * pairs * rhs, rhs), :]
        high = coef_ref[pl.ds((at * pairs + pairs - 1) * rhs, rhs), :]
        send(low, high, comps * side + at * rhs, rhs, 1)
    top = sent_ref[pl.ds(comps * line + block, sent_ref.shape[0] - comps * line - block), :]
    if merged:
        top = top + got[pl.ds(comps * line + block, top.shape[0]), :]
    even_ref[pl.ds(comps * side + 3 * rows * rhs, top.shape[0]), :] = top


def rows_kernel(rows, cols, rhs, leaf,
                mask_any, above_ref, below_ref, targets, factors, near_in,
                near_ref,
                near_mask, feat, spread, values, sems):
    copies = start_all([(mask_any, near_mask)], sems)
    source_map = source_choice()
    for ref, line in ((above_ref, 0), (below_ref, 1)):
        fill(feat, ref, 2 * cols)
        for col in range(cols):
            place(ref, feat, spread, values, source_map, rhs, col, cols, 2 * cols, line * cols + col)
    copies[0].wait()
    for at in range(rows * cols):
        row, col = at // cols, at % cols
        total = near_in[at]
        for slot in range(9):
            to_row, to_col = row + slot // 3 - 1, col + slot % 3 - 1
            if not 0 <= to_row < rows and 0 <= to_col < cols:
                other = (0 if to_row < 0 else cols) + to_col
                total = total + tile_product(
                    spread[other], step_target(targets, factors, at, slot), values[other], near_mask[row, col, slot] != 0
                )
        near_ref[at] = total


def far_kernel(rows, cols, rhs, rank, far_list,
               far_any, left_ref, right_ref, coef_ref, coupling_any, basis_ref,
               far_ref,
               far_mask, coupling, dup, wide_hi, wide_lo, sems):
    copies = start_all([(far_any, far_mask), (coupling_any, coupling)], sems)
    leaves = rows * cols
    low = lax.broadcasted_iota(jnp.int32, (rhs, 2 * rank), 1) < rank
    pairs = cols // 2
    for line in range(rows + 4):
        for pair in range(pairs + 2):
            if pair == 0:
                both = left_ref[pl.ds(line * rhs, rhs), :]
            elif pair == pairs + 1:
                both = right_ref[pl.ds(line * rhs, rhs), :]
            else:
                both = coef_ref[pl.ds((line * pairs + pair - 1) * rhs, rhs), :]
            turned = pltpu.roll(both, rank, 1)
            at = line * (cols + 4) + 2 * pair
            dup[at] = jnp.where(low, both, turned)
            dup[at + 1] = jnp.where(low, turned, both)
    copies[0].wait()
    for row in range(rows):
        for col in range(cols):
            at = row * cols + col
            for chunk in range(len(far_list) // 2):
                parts = []
                for slot in (2 * chunk, 2 * chunk + 1):
                    down_step, right_step = far_list[slot]
                    part = dup[(row + 2 + down_step) * (cols + 4) + col + 2 + right_step]
                    parts.append(jnp.where(far_mask[row, col, slot] != 0, part, 0.0))
                hi, lo = split(jnp.where(low, parts[0], parts[1]))
                wide_hi[pl.ds(at * rhs, rhs), pl.ds(chunk * 2 * rank, 2 * rank)] = hi
                wide_lo[pl.ds(at * rhs, rhs), pl.ds(chunk * 2 * rank, 2 * rank)] = lo
    copies[1].wait()
    ch, cl = split(jnp.concatenate([coupling[slot] for slot in range(len(far_list))], 1))
    far = dot(wide_hi[...], ch, NT) + dot(wide_hi[...], cl, NT) + dot(wide_lo[...], ch, NT)
    for at in range(leaves):
        both = basis_ref[at]
        fh, fl = split(far[at * rhs : (at + 1) * rhs])
        far_ref[at] = dot(fh, both[:rank]) + dot(fl, both[:rank]) + dot(fh, both[rank:])


def side_kernel(rows, cols, rhs, leaf,
                mask_any, left_ref, right_ref, targets, factors, near_ref, far_ref,
                base_ref,
                near_mask, feat, spread, values, sems):
    copies = start_all([(mask_any, near_mask)], sems)
    source_map = source_choice()
    side = 2 * (rows + 2)
    for ref, first in ((left_ref, 0), (right_ref, rows + 2)):
        fill(feat, ref, side)
        for line in range(rows + 2):
            place(ref, feat, spread, values, source_map, rhs, 2 * line, 1, side, first + line)
    copies[0].wait()
    scale = 1.0 / (3.0 * float(leaf) ** 0.5)
    for at in range(rows * cols):
        row, col = at // cols, at % cols
        total = near_ref[at]
        for slot in range(9):
            to_row, to_col = row + slot // 3 - 1, col + slot % 3 - 1
            if not 0 <= to_col < cols:
                other = (0 if to_col < 0 else rows + 2) + to_row + 1
                total = total + tile_product(
                    spread[other], step_target(targets, factors, at, slot), values[other], near_mask[row, col, slot] != 0
                )
        base_ref[at] = total * scale + far_ref[at]


def finish_kernel(rows, cols, rhs, rank, nodes, owner_ref, top_ref, down_ref, base_ref, out_ref):
    lines = 2 * rows * cols
    high = (lax.broadcasted_iota(jnp.int32, (rhs, 2 * rank), 1) >= rank).astype(jnp.int32)
    owner = owner_ref[...] - high
    chosen = jnp.zeros((rhs, 2 * rank), F32)
    for pair in range(nodes // 2):
        chosen = jnp.where(owner == 2 * pair, top_ref[pl.ds(pair * rhs, rhs), :], chosen)
    local = (chosen + pltpu.roll(chosen, rank, 1))[:, :rank]
    hi, lo = split(local)
    stacked = jnp.concatenate([hi, lo], 0)
    for at in range(rows * cols):
        first = dot(stacked, down_ref[at, pl.ds(0, rank)])
        second = dot(hi, down_ref[at, pl.ds(rank, rank)])
        start = (at // cols) * 2 * cols + at % cols
        put_strided(out_ref, start, cols, rhs, lines, base_ref[at] + (first[:rhs] + first[rhs:] + second))


VMEM = pl.BlockSpec(memory_space=pltpu.VMEM)
SMEM = pl.BlockSpec(memory_space=pltpu.SMEM)
ANY = pl.BlockSpec(memory_space=pltpu.HBM)


def lanes(x):
    x = x.reshape(x.shape[:-1] + (2, 128))
    return jnp.swapaxes(x, -3, -2).reshape(-1, 128)


def on_device(
    vectors,
    leaf_order,
    offsets,
    near_mask,
    far_mask,
    basis,
    transfer,
    coupling,
    top_coupling,
    cluster_owner,
):
    rhs, rows, cols, leaf = vectors.shape
    rank = basis.shape[2]
    nodes = top_coupling.shape[0]
    leaves = rows * cols
    n_row, n_col = lax.axis_size("row"), lax.axis_size("col")
    devices = n_row * n_col
    col_even = lax.axis_index("col") % 2 == 0
    comps = 3 + rhs
    near_rows = comps * 2 * cols

    def params():
        return pltpu.CompilerParams(vmem_limit_bytes=12 * 1024 * 1024)

    def grid_perm(step):
        return [
            (r * n_col + c, t[0] * n_col + t[1])
            for r in range(n_row)
            for c in range(n_col)
            for t in [step(r, c)]
            if t is not None
        ]

    def permute(x, step):
        return lax.ppermute(x, AXES, grid_perm(step))

    def sibling(r, c):
        return (r ^ 1, c)

    def odd_rows(r, c):
        t = r + 1 if r % 2 else r - 1
        return (t, c) if 0 <= t < n_row else None

    def other_row(r, c):
        return (n_row - 1 - r, c)

    def even_cols(r, c):
        return (r, c ^ 1)

    def odd_cols(r, c):
        t = c + 1 if c % 2 else c - 1
        return (r, t) if 0 <= t < n_col else None

    def doubled(x, step):
        return x + lax.ppermute(x, AXES, [(i, i ^ step) for i in range(devices)])

    def in_hbm(x):
        return pltpu.with_memory_space_constraint(x, pltpu.HBM)

    vec = lanes(vectors)
    vec_sib = permute(vec, sibling)
    transfer2 = transfer.reshape(leaves * rank, rank)
    pos, coef, basis_own, sent, owner = pl.pallas_call(
        functools.partial(prepare_kernel, rows, cols, rhs, rank, leaf, nodes),
        out_shape=(
            jax.ShapeDtypeStruct((3 * 2 * leaves, 128), F32),
            jax.ShapeDtypeStruct((leaves // 2 * rhs, 2 * rank), F32),
            jax.ShapeDtypeStruct((leaves, 2 * rank, leaf), BF16),
            jax.ShapeDtypeStruct((near_rows + (leaves + nodes) // 2 * rhs, 128), F32),
            jax.ShapeDtypeStruct((rhs, 2 * rank), jnp.int32),
        ),
        in_specs=[SMEM] + [ANY] * 6,
        out_specs=(VMEM,) * 5,
        scratch_shapes=[
            pltpu.VMEM((rhs * 2 * leaves, 128), F32),
            pltpu.VMEM((2 * leaves, 128), jnp.int32),
            pltpu.VMEM((3 * 2 * leaves, 128), F32),
            pltpu.VMEM((leaves, rank, leaf), F32),
            pltpu.VMEM((leaves * rank, rank), F32),
            pltpu.VMEM((nodes, rank, rank), F32),
            pltpu.VMEM((FEATS * 2 * leaves, 128), F32),
            pltpu.VMEM((nodes * rank, rank), F32),
            pltpu.SemaphoreType.DMA((6,)),
        ],
        compiler_params=params(),
        name="prepare",
    )(
        cluster_owner,
        in_hbm(vec),
        in_hbm(lanes(leaf_order)),
        in_hbm(lanes(offsets)),
        in_hbm(basis.reshape(leaves, rank, leaf)),
        in_hbm(transfer2),
        in_hbm(top_coupling),
    )

    merged = n_row == 4
    halo_rows = near_rows + coef.shape[0]
    if merged:
        got = permute(sent, other_row)
    else:
        got = permute(sent[:halo_rows], odd_rows)
    pos_sib = permute(pos, sibling)
    coef_sib = permute(coef, sibling)

    near_slots = in_hbm(jnp.transpose(near_mask, (1, 2, 0)))
    far_slots = in_hbm(jnp.transpose(far_mask, (1, 2, 0)))
    near_table = pltpu.SMEM((rows, cols, 9), jnp.int32)
    near_shape = jax.ShapeDtypeStruct((leaves, rhs, leaf), F32)
    near, targets, factors = pl.pallas_call(
        functools.partial(own_kernel, rows, cols, rhs, rank, leaf),
        out_shape=(
            near_shape,
            jax.ShapeDtypeStruct((leaves, K, leaf), BF16),
            jax.ShapeDtypeStruct((9, K, 128), BF16),
        ),
        in_specs=[ANY, VMEM, VMEM],
        out_specs=(VMEM,) * 3,
        scratch_shapes=[
            near_table,
            pltpu.VMEM((FEATS * 2 * leaves, 128), F32),
            pltpu.VMEM((leaves, leaf, K), BF16),
            pltpu.VMEM((leaves, 2 * rhs, leaf), BF16),
            pltpu.SemaphoreType.DMA((1,)),
        ],
        compiler_params=params(),
        name="own",
    )(near_slots, vec, pos)

    got, near = lax.optimization_barrier((got, near))
    side_rows = comps * (rows + 2) * 2
    column_rows = side_rows + 3 * rows * rhs
    top_rows = nodes // 2 * rhs
    above, below, coef_mid, even_sent, odd_sent = pl.pallas_call(
        functools.partial(gather_kernel, rows, cols, rhs, n_row, merged),
        out_shape=tuple(
            jax.ShapeDtypeStruct((count, 128), F32)
            for count in (near_rows, near_rows, 3 * coef.shape[0], column_rows + top_rows, column_rows)
        ),
        in_specs=[ANY] * 5 + [VMEM] * 3,
        out_specs=(VMEM,) * 5,
        scratch_shapes=[
            pltpu.VMEM(vec.shape, F32),
            pltpu.VMEM(vec.shape, F32),
            pltpu.VMEM(pos.shape, F32),
            pltpu.VMEM(coef.shape, F32),
            pltpu.VMEM(got.shape, F32),
            pltpu.SemaphoreType.DMA((5,)),
        ],
        compiler_params=params(),
        name="gather",
    )(vec, vec_sib, pos_sib, coef_sib, got, pos, coef, sent)

    got_even = permute(even_sent, even_cols)
    got_odd = permute(odd_sent, odd_cols)

    near = pl.pallas_call(
        functools.partial(rows_kernel, rows, cols, rhs, leaf),
        out_shape=near_shape,
        in_specs=[ANY] + [VMEM] * 5,
        out_specs=VMEM,
        scratch_shapes=[
            near_table,
            pltpu.VMEM((FEATS * 2 * cols, 128), F32),
            pltpu.VMEM((2 * cols, leaf, K), BF16),
            pltpu.VMEM((2 * cols, 2 * rhs, leaf), BF16),
            pltpu.SemaphoreType.DMA((1,)),
        ],
        compiler_params=params(),
        name="rows",
    )(near_slots, above, below, targets, factors, near)

    top, near = lax.optimization_barrier((even_sent[column_rows:] + got_even[column_rows:], near))
    left = jnp.where(col_even, got_odd, got_even[:column_rows])
    right = jnp.where(col_even, got_even[:column_rows], got_odd)

    down = pl.pallas_call(
        functools.partial(down_kernel, leaves, rank),
        out_shape=jax.ShapeDtypeStruct((leaves, 2 * rank, leaf), BF16),
        in_specs=[VMEM, VMEM],
        out_specs=VMEM,
        compiler_params=params(),
        name="down",
    )(basis_own, transfer2)

    steps = [n_col << k for k in range(1 if merged else n_row.bit_length() - 1)]
    steps += [2 << k for k in range(n_col.bit_length() - 2)]
    top = doubled(top, steps[0])
    top, down = lax.optimization_barrier((top, down))

    far = pl.pallas_call(
        functools.partial(far_kernel, rows, cols, rhs, rank, far_offsets()),
        out_shape=near_shape,
        in_specs=[ANY] + [VMEM] * 3 + [ANY, VMEM],
        out_specs=VMEM,
        scratch_shapes=[
            pltpu.SMEM((rows, cols, 16), jnp.int32),
            pltpu.VMEM(coupling.shape, F32),
            pltpu.VMEM(((rows + 4) * (cols + 4), rhs, 2 * rank), F32),
            pltpu.VMEM((leaves * rhs, 16 * rank), BF16),
            pltpu.VMEM((leaves * rhs, 16 * rank), BF16),
            pltpu.SemaphoreType.DMA((2,)),
        ],
        compiler_params=params(),
        name="far",
    )(far_slots, left[side_rows:], right[side_rows:], coef_mid, in_hbm(coupling), basis_own)

    top = doubled(top, steps[1])
    top, far = lax.optimization_barrier((top, far))
    for step in steps[2:]:
        top = doubled(top, step)

    sides = 2 * (rows + 2)
    base = pl.pallas_call(
        functools.partial(side_kernel, rows, cols, rhs, leaf),
        out_shape=near_shape,
        in_specs=[ANY] + [VMEM] * 6,
        out_specs=VMEM,
        scratch_shapes=[
            near_table,
            pltpu.VMEM((FEATS * sides, 128), F32),
            pltpu.VMEM((sides, leaf, K), BF16),
            pltpu.VMEM((sides, 2 * rhs, leaf), BF16),
            pltpu.SemaphoreType.DMA((1,)),
        ],
        compiler_params=params(),
        name="side",
    )(near_slots, left[:side_rows], right[:side_rows], targets, factors, near, far)

    out = pl.pallas_call(
        functools.partial(finish_kernel, rows, cols, rhs, rank, nodes),
        out_shape=jax.ShapeDtypeStruct((rhs * 2 * leaves, 128), F32),
        in_specs=[VMEM] * 4,
        out_specs=VMEM,
        compiler_params=params(),
        name="finish",
    )(owner, top, down, base)
    out = jnp.swapaxes(out.reshape(rhs, rows, 2, cols, 128), 2, 3)
    return out.reshape(rhs, rows, cols, leaf)


def solution(mesh):
    in_specs = (
        P(None, "row", "col", None),
        P("row", "col", None),
        P(None, "row", "col", None),
        P(None, "row", "col"),
        P(None, "row", "col"),
        P("row", "col", None, None),
        P("row", "col", None, None),
        P(),
        P(),
        P("row", "col"),
    )
    out_specs = P(None, "row", "col", None)
    return jax.shard_map(
        on_device, mesh=mesh, in_specs=in_specs, out_specs=out_specs, check_vma=False
    )
```

```python
import functools

import jax
import jax.numpy as jnp
import numpy as np
from jax import lax
from jax.experimental import pallas as pl
from jax.experimental.pallas import tpu as pltpu
from jax.sharding import PartitionSpec as P

softening = 0.01
F32 = jnp.float32
BF16 = jnp.bfloat16
AXES = ("row", "col")
NT = (((1,), (1,)), ((), ()))
TN = (((0,), (0,)), ((), ()))
NN = (((1,), (0,)), ((), ()))
FEATS = 16
K = 32


def far_offsets():
    found = []
    for down_step in range(-2, 3):
        for right_step in range(-2, 3):
            if max(abs(down_step), abs(right_step)) == 2:
                found.append((down_step, right_step))
    return found


def dot(a, b, dims=NN):
    return lax.dot_general(a, b, dims, preferred_element_type=F32)


def split(x):
    hi = x.astype(BF16)
    lo = (x - hi.astype(F32)).astype(BF16)
    return hi, lo


def dot_parts(a, b_hi, b_lo, dims=NN):
    rows = a.shape[0]
    both = jnp.concatenate(split(a), 0)
    first, second = dot(both, b_hi, dims), dot(both, b_lo, dims)
    return (first[:rows] + first[rows:]) + (second[:rows] + second[rows:])


def dot3(a, b, dims=NN):
    return dot_parts(a, *split(b), dims)


def strided(ref, start, half, count, stride):
    first = ref[pl.ds(start, count, stride=stride), :]
    second = ref[pl.ds(start + half, count, stride=stride), :]
    return jnp.concatenate([first, second], 1)


def put_strided(ref, start, half, count, stride, x):
    ref[pl.ds(start, count, stride=stride), :] = x[:, :128]
    ref[pl.ds(start + half, count, stride=stride), :] = x[:, 128:]


def products(slot):
    step = (slot // 3 - 1, slot % 3 - 1)
    one = 9
    found = []
    for comp in range(3):
        for mine in range(2):
            for other in range(2):
                found.append((2 * comp + mine, 2 * comp + other, -2.0))
    for part in range(3):
        found.append((6 + part, one, 1.0))
        found.append((one, 6 + part, 1.0))
    for comp in range(2):
        for part in range(2):
            found.append((2 * comp + part, one, 2.0 * step[comp]))
            found.append((one, 2 * comp + part, -2.0 * step[comp]))
    rest = np.float32(softening)
    for _ in range(3):
        part = np.float32(np.asarray(rest, jnp.bfloat16))
        found.append((one, one, float(part)))
        rest = np.float32(rest - part)
    found.append((one, one, float(step[0] ** 2 + step[1] ** 2)))
    return found


def source_choice():
    feat = lax.broadcasted_iota(jnp.int32, (FEATS, K), 0)
    at = lax.broadcasted_iota(jnp.int32, (FEATS, K), 1)
    chosen = jnp.zeros((FEATS, K), F32)
    for i, (mine, _, _) in enumerate(products(0)):
        chosen = jnp.where((at == i) & (feat == mine), 1.0, chosen)
    return chosen.astype(BF16)


def target_choice():
    at = lax.broadcasted_iota(jnp.int32, (K, FEATS), 0)
    feat = lax.broadcasted_iota(jnp.int32, (K, FEATS), 1)
    chosen = jnp.zeros((K, FEATS), F32)
    for i, (_, other, _) in enumerate(products(0)):
        chosen = jnp.where((at == i) & (feat == other), 1.0, chosen)
    return chosen.astype(BF16)


def put_factors(factors):
    at = lax.broadcasted_iota(jnp.int32, (K, 128), 0)
    for slot in range(9):
        factor = jnp.zeros((K, 128), F32)
        for i, (_, _, value) in enumerate(products(slot)):
            if value:
                factor = jnp.where(at == i, value, factor)
        factors[slot] = factor.astype(BF16)


def start_all(pairs, sems):
    copies = [pltpu.make_async_copy(src, dst, sems.at[i]) for i, (src, dst) in enumerate(pairs)]
    for copy in copies:
        copy.start()
    return copies


def prepare_kernel(rows, cols, rhs, rank, leaf, nodes,
                   owner_ref, vec_any, order_any, off_any, basis_any, transfer_any, table_any,
                   pair_ref, basis_out, sent_ref, owner_out,
                   vec, order, off, basis, transfer, table, feat, rolled, sems):
    leaves = rows * cols
    lines = 2 * leaves
    copies = start_all(
        [(order_any, order), (off_any, off), (basis_any, basis), (vec_any, vec), (transfer_any, transfer), (table_any, table)],
        sems,
    )
    copies[0].wait()
    copies[1].wait()
    for comp in range(3):
        u = off[pl.ds(comp * lines, lines), :] - 0.5
        if comp == 2:
            u = u * 0.25
        hi = u.astype(BF16).astype(F32)
        feat[pl.ds(2 * comp * lines, lines), :] = hi
        feat[pl.ds((2 * comp + 1) * lines, lines), :] = (u - hi).astype(BF16).astype(F32)
    feat[pl.ds(6 * lines, 10 * lines), :] = jnp.zeros((10 * lines, 128), F32)
    copies[2].wait()
    copies[3].wait()
    spots = lax.broadcasted_iota(jnp.int32, (leaf, leaf), 0)
    offs = []
    for at in range(leaves):
        start = (at // cols) * 2 * cols + at % cols
        own_order = jnp.concatenate([order[pl.ds(start, 1), :], order[pl.ds(start + cols, 1), :]], 1)
        chosen = (jnp.broadcast_to(own_order, (leaf, leaf)) == spots).astype(F32).astype(BF16)
        bh, bl = split(basis[at])
        own = strided(feat, start, cols, FEATS, lines).astype(BF16)
        moved = dot(jnp.concatenate([bh, bl, own], 0), chosen, NT)
        basis_out[at] = moved[: 2 * rank].astype(BF16)
        offs.append(moved[2 * rank :])
    coefs = []
    for at in range(leaves):
        start = (at // cols) * 2 * cols + at % cols
        xh, xl = split(strided(vec, start, cols, rhs, lines))
        four = dot(jnp.concatenate([xh, xl], 0), basis_out[at], NT)
        coefs.append(four[:rhs, :rank] + four[:rhs, rank:] + four[rhs:, :rank] + four[rhs:, rank:])
    for at in range(leaves):
        start = (at // cols) * 2 * cols + at % cols
        for comp in range(3):
            line = offs[at][2 * comp : 2 * comp + 1] + offs[at][2 * comp + 1 : 2 * comp + 2]
            pair_ref[pl.ds(comp * lines + start, 1), :] = line[:, :128]
            pair_ref[pl.ds(comp * lines + start + cols, 1), :] = line[:, 128:]
    wide = [jnp.concatenate([coefs[2 * p], coefs[2 * p + 1]], 1) for p in range(leaves // 2)]
    row = jnp.where(lax.rem(lax.axis_index("row"), 2) == 0, 0, (rows - 1) * 2 * cols)
    for comp in range(3 + rhs):
        ref, first = (pair_ref, comp) if comp < 3 else (vec, comp - 3)
        sent_ref[pl.ds(comp * 2 * cols, 2 * cols), :] = ref[pl.ds(pl.multiple_of(first * lines + row, 2 * cols), 2 * cols), :]
    near_rows = (3 + rhs) * 2 * cols
    for p in range(leaves // 2):
        pair_ref[pl.ds(3 * lines + p * rhs, rhs), :] = wide[p]
        sent_ref[pl.ds(near_rows + p * rhs, rhs), :] = wide[p]
    copies[4].wait()
    cluster = dot3(jnp.concatenate(wide, 1), transfer[...])
    copies[5].wait()
    owner = owner_ref[0, 0]
    owner_out[...] = jnp.full(owner_out.shape, owner, jnp.int32)
    for node in range(nodes):
        gap = lax.rem(node - owner + nodes, nodes)
        rolled[pl.ds(node * rank, rank), :] = table[gap] * jnp.where(gap == 0, 0.0, 1.0)
    terms = dot3(cluster, rolled[...], NT)
    for pair in range(nodes // 2):
        sent_ref[pl.ds(near_rows + (leaves // 2 + pair) * rhs, rhs), :] = terms[:, pair * 2 * rank : (pair + 1) * 2 * rank]


def fill(into, ref, lines):
    total = jnp.zeros((lines, 128), F32)
    for comp in range(3):
        u = ref[pl.ds(comp * lines, lines), :]
        hi = u.astype(BF16).astype(F32)
        into[pl.ds(2 * comp * lines, lines), :] = hi
        into[pl.ds((2 * comp + 1) * lines, lines), :] = u - hi
        total = total + u * u
    for part in range(3):
        hi = total.astype(BF16).astype(F32)
        into[pl.ds((6 + part) * lines, lines), :] = hi
        total = total - hi
    into[pl.ds(9 * lines, lines), :] = jnp.ones((lines, 128), F32)
    into[pl.ds(10 * lines, 6 * lines), :] = jnp.zeros((6 * lines, 128), F32)


def step_target(targets, factors, at, slot):
    factor = factors[slot]
    return targets[at] * jnp.concatenate([factor, factor], 1)


def place(points, feats, spread, values, source_map, rhs, start, half, stride, at):
    own = strided(feats, start, half, FEATS, stride).astype(BF16)
    spread[at] = dot(own, source_map, TN).astype(BF16)
    xh, xl = split(strided(points, 3 * stride + start, half, rhs, stride))
    values[at] = jnp.concatenate([xh, xl], 0)


def tile_product(spread, target, values, keep):
    kh, kl = split(lax.rsqrt(dot(spread, target)))
    x = jnp.where(keep, values, jnp.zeros_like(values))
    rhs = x.shape[0] // 2
    first, second = dot(x, kh), dot(x, kl)
    return (first[:rhs] + first[rhs:]) + (second[:rhs] + second[rhs:])


def own_kernel(rows, cols, rhs, rank, leaf,
               mask_any, vec, pos_ref,
               near_ref, targets, factors,
               near_mask, feat, spread, values, sems):
    copies = start_all([(mask_any, near_mask)], sems)
    leaves = rows * cols
    lines = 2 * leaves
    fill(feat, pos_ref, lines)
    put_factors(factors)
    source_map, target_map = source_choice(), target_choice()
    for at in range(leaves):
        start = (at // cols) * 2 * cols + at % cols
        own = strided(feat, start, cols, FEATS, lines).astype(BF16)
        spread[at] = dot(own, source_map, TN).astype(BF16)
    for at in range(leaves):
        start = (at // cols) * 2 * cols + at % cols
        own = strided(feat, start, cols, FEATS, lines).astype(BF16)
        targets[at] = dot(target_map, own).astype(BF16)
    for at in range(leaves):
        start = (at // cols) * 2 * cols + at % cols
        xh, xl = split(strided(vec, start, cols, rhs, lines))
        values[at] = jnp.concatenate([xh, xl], 0)
    copies[0].wait()
    for at in range(leaves):
        row, col = at // cols, at % cols
        total = jnp.zeros((rhs, leaf), F32)
        for slot in range(9):
            to_row, to_col = row + slot // 3 - 1, col + slot % 3 - 1
            if 0 <= to_row < rows and 0 <= to_col < cols:
                other = to_row * cols + to_col
                total = total + tile_product(
                    spread[other], step_target(targets, factors, at, slot), values[other], near_mask[row, col, slot] != 0
                )
        near_ref[at] = total


def down_kernel(leaves, rank, basis_ref, transfer, down_ref):
    for at in range(leaves):
        both = basis_ref[at]
        th, tl = split(transfer[pl.ds(at * rank, rank), :])
        moved = dot(th, both[:rank], TN) + dot(tl, both[:rank], TN) + dot(th, both[rank:], TN)
        gh, gl = split(moved)
        down_ref[at] = jnp.concatenate([gh, gl], 0)


def gather_kernel(rows, cols, rhs, n_row,
                  vec_any, vec_sib_any, pair_sib_any, got_any, pair,
                  above_ref, below_ref, coef_ref, even_ref, odd_ref,
                  vec, vec_sib, pair_sib, got, sems):
    copies = start_all(
        [(vec_any, vec), (vec_sib_any, vec_sib), (pair_sib_any, pair_sib), (got_any, got)], sems
    )
    comps = 3 + rhs
    lines = 2 * rows * cols
    line = 2 * cols
    my_row = lax.axis_index("row")
    row_even = lax.rem(my_row, 2) == 0
    col_even = lax.rem(lax.axis_index("col"), 2) == 0
    beyond = jnp.where(row_even, my_row > 0, my_row < n_row - 1)
    for copy in copies:
        copy.wait()
    row = jnp.where(row_even, 0, (rows - 1) * line)
    for comp in range(comps):
        ref, first = (pair_sib, comp) if comp < 3 else (vec_sib, comp - 3)
        near = ref[pl.ds(pl.multiple_of(first * lines + row, line), line), :]
        mine = pl.ds(comp * line, line)
        far = jnp.where(beyond, got[mine, :], 0.0)
        above_ref[mine, :] = jnp.where(row_even, far, near)
        below_ref[mine, :] = jnp.where(row_even, near, far)
    block = rows * cols // 2 * rhs
    own_coef = pl.ds(3 * lines, block)
    near = pair_sib[own_coef, :]
    far = jnp.where(beyond, got[pl.ds(comps * line, block), :], 0.0)
    coef_ref[pl.ds(0, block), :] = jnp.where(row_even, far, near)
    coef_ref[pl.ds(block, block), :] = pair[own_coef, :]
    coef_ref[pl.ds(2 * block, block), :] = jnp.where(row_even, near, far)

    def send(low, high, start, count, stride):
        where = pl.ds(start, count) if stride == 1 else pl.ds(start, count, stride=stride)
        even_ref[where, :] = jnp.where(col_even, high, low)
        odd_ref[where, :] = jnp.where(col_even, low, high)

    def column(ref, start, count, stride):
        return [ref[pl.ds(start + at, count, stride=stride), :] for at in (0, cols - 1)]

    side = 2 * (rows + 2)
    for half in range(2):
        send(*column(above_ref, half * cols, comps, line), half, comps, side)
        send(*column(below_ref, half * cols, comps, line), 2 * (rows + 1) + half, comps, side)
        for r in range(rows):
            to = 2 * (r + 1) + half
            send(*column(pair, (2 * r + half) * cols, 3, lines), to, 3, side)
            send(*column(vec, (2 * r + half) * cols, rhs, lines), 3 * side + to, rhs, side)
    pairs = cols // 2
    for at in range(3 * rows):
        low = coef_ref[pl.ds(at * pairs * rhs, rhs), :]
        high = coef_ref[pl.ds((at * pairs + pairs - 1) * rhs, rhs), :]
        send(low, high, comps * side + at * rhs, rhs, 1)


def rows_kernel(rows, cols, rhs, leaf,
                mask_any, above_ref, below_ref, targets, factors, near_in,
                near_ref,
                near_mask, feat, spread, values, sems):
    copies = start_all([(mask_any, near_mask)], sems)
    source_map = source_choice()
    for ref, line in ((above_ref, 0), (below_ref, 1)):
        fill(feat, ref, 2 * cols)
        for col in range(cols):
            place(ref, feat, spread, values, source_map, rhs, col, cols, 2 * cols, line * cols + col)
    copies[0].wait()
    for at in range(rows * cols):
        row, col = at // cols, at % cols
        total = near_in[at]
        for slot in range(9):
            to_row, to_col = row + slot // 3 - 1, col + slot % 3 - 1
            if not 0 <= to_row < rows and 0 <= to_col < cols:
                other = (0 if to_row < 0 else cols) + to_col
                total = total + tile_product(
                    spread[other], step_target(targets, factors, at, slot), values[other], near_mask[row, col, slot] != 0
                )
        near_ref[at] = total


def far_kernel(rows, cols, rhs, rank, far_list,
               far_any, left_ref, right_ref, coef_ref, coupling_any, basis_ref,
               far_ref,
               far_mask, coupling, dup, wide, sems):
    copies = start_all([(far_any, far_mask), (coupling_any, coupling)], sems)
    leaves = rows * cols
    low = lax.broadcasted_iota(jnp.int32, (rhs, 2 * rank), 1) < rank
    pairs = cols // 2
    for line in range(rows + 4):
        for pair in range(pairs + 2):
            if pair == 0:
                both = left_ref[pl.ds(line * rhs, rhs), :]
            elif pair == pairs + 1:
                both = right_ref[pl.ds(line * rhs, rhs), :]
            else:
                both = coef_ref[pl.ds((line * pairs + pair - 1) * rhs, rhs), :]
            turned = pltpu.roll(both, rank, 1)
            at = line * (cols + 4) + 2 * pair
            dup[at] = jnp.where(low, both, turned)
            dup[at + 1] = jnp.where(low, turned, both)
    copies[0].wait()
    for row in range(rows):
        for col in range(cols):
            at = row * cols + col
            for chunk in range(len(far_list) // 2):
                parts = []
                for slot in (2 * chunk, 2 * chunk + 1):
                    down_step, right_step = far_list[slot]
                    part = dup[(row + 2 + down_step) * (cols + 4) + col + 2 + right_step]
                    parts.append(jnp.where(far_mask[row, col, slot] != 0, part, 0.0))
                hi, lo = split(jnp.where(low, parts[0], parts[1]))
                wide[pl.ds(at * rhs, rhs), pl.ds(chunk * 2 * rank, 2 * rank)] = hi
                wide[pl.ds((leaves + at) * rhs, rhs), pl.ds(chunk * 2 * rank, 2 * rank)] = lo
    copies[1].wait()
    both = jnp.concatenate(split(jnp.concatenate([coupling[slot] for slot in range(len(far_list))], 1)), 0)
    four = dot(wide[...], both, NT)
    half = leaves * rhs
    far = (four[:half, :rank] + four[half:, :rank]) + (four[:half, rank:] + four[half:, rank:])
    for at in range(leaves):
        both = basis_ref[at]
        far_ref[at] = dot_parts(far[at * rhs : (at + 1) * rhs], both[:rank], both[rank:])


def side_kernel(rows, cols, rhs, leaf,
                mask_any, left_ref, right_ref, targets, factors, near_ref, far_ref,
                base_ref,
                near_mask, feat, spread, values, sems):
    copies = start_all([(mask_any, near_mask)], sems)
    source_map = source_choice()
    side = 2 * (rows + 2)
    for ref, first in ((left_ref, 0), (right_ref, rows + 2)):
        fill(feat, ref, side)
        for line in range(rows + 2):
            place(ref, feat, spread, values, source_map, rhs, 2 * line, 1, side, first + line)
    copies[0].wait()
    scale = 1.0 / (3.0 * float(leaf) ** 0.5)
    for at in range(rows * cols):
        row, col = at // cols, at % cols
        total = near_ref[at]
        for slot in range(9):
            to_row, to_col = row + slot // 3 - 1, col + slot % 3 - 1
            if not 0 <= to_col < cols:
                other = (0 if to_col < 0 else rows + 2) + to_row + 1
                total = total + tile_product(
                    spread[other], step_target(targets, factors, at, slot), values[other], near_mask[row, col, slot] != 0
                )
        base_ref[at] = total * scale + far_ref[at]


def finish_kernel(rows, cols, rhs, rank, nodes, owner_ref, top_ref, down_ref, base_ref, out_ref):
    lines = 2 * rows * cols
    high = (lax.broadcasted_iota(jnp.int32, (rhs, 2 * rank), 1) >= rank).astype(jnp.int32)
    owner = owner_ref[...] - high
    chosen = jnp.zeros((rhs, 2 * rank), F32)
    for pair in range(nodes // 2):
        chosen = jnp.where(owner == 2 * pair, top_ref[pl.ds(pair * rhs, rhs), :], chosen)
    local = (chosen + pltpu.roll(chosen, rank, 1))[:, :rank]
    for at in range(rows * cols):
        down = dot_parts(local, down_ref[at, pl.ds(0, rank)], down_ref[at, pl.ds(rank, rank)])
        start = (at // cols) * 2 * cols + at % cols
        put_strided(out_ref, start, cols, rhs, lines, base_ref[at] + down)


VMEM = pl.BlockSpec(memory_space=pltpu.VMEM)
SMEM = pl.BlockSpec(memory_space=pltpu.SMEM)
ANY = pl.BlockSpec(memory_space=pltpu.HBM)


def lanes(x):
    x = x.reshape(x.shape[:-1] + (2, 128))
    return jnp.swapaxes(x, -3, -2).reshape(-1, 128)


def on_device(
    vectors,
    leaf_order,
    offsets,
    near_mask,
    far_mask,
    basis,
    transfer,
    coupling,
    top_coupling,
    cluster_owner,
):
    rhs, rows, cols, leaf = vectors.shape
    rank = basis.shape[2]
    nodes = top_coupling.shape[0]
    leaves = rows * cols
    n_row, n_col = lax.axis_size("row"), lax.axis_size("col")
    devices = n_row * n_col
    col_even = lax.axis_index("col") % 2 == 0
    comps = 3 + rhs
    near_rows = comps * 2 * cols
    coef_rows = leaves // 2 * rhs
    top_rows = nodes // 2 * rhs
    halo_rows = near_rows + coef_rows

    def params():
        return pltpu.CompilerParams(vmem_limit_bytes=12 * 1024 * 1024)

    def grid_perm(step):
        return [
            (r * n_col + c, t[0] * n_col + t[1])
            for r in range(n_row)
            for c in range(n_col)
            for t in [step(r, c)]
            if t is not None
        ]

    def permute(x, step):
        return lax.ppermute(x, AXES, grid_perm(step))

    def sibling(r, c):
        return (r ^ 1, c)

    def odd_rows(r, c):
        t = r + 1 if r % 2 else r - 1
        return (t, c) if 0 <= t < n_row else None

    def other_row(r, c):
        return (n_row - 1 - r, c)

    def even_cols(r, c):
        return (r, c ^ 1)

    def odd_cols(r, c):
        t = c + 1 if c % 2 else c - 1
        return (r, t) if 0 <= t < n_col else None

    def doubled(x, step):
        return x + lax.ppermute(x, AXES, [(i, i ^ step) for i in range(devices)])

    def in_hbm(x):
        return pltpu.with_memory_space_constraint(x, pltpu.HBM)

    vec = lanes(vectors)
    transfer2 = transfer.reshape(leaves * rank, rank)
    pair, basis_own, sent, owner = pl.pallas_call(
        functools.partial(prepare_kernel, rows, cols, rhs, rank, leaf, nodes),
        out_shape=(
            jax.ShapeDtypeStruct((3 * 2 * leaves + coef_rows, 128), F32),
            jax.ShapeDtypeStruct((leaves, 2 * rank, leaf), BF16),
            jax.ShapeDtypeStruct((halo_rows + top_rows, 128), F32),
            jax.ShapeDtypeStruct((rhs, 2 * rank), jnp.int32),
        ),
        in_specs=[SMEM] + [ANY] * 6,
        out_specs=(VMEM,) * 4,
        scratch_shapes=[
            pltpu.VMEM((rhs * 2 * leaves, 128), F32),
            pltpu.VMEM((2 * leaves, 128), jnp.int32),
            pltpu.VMEM((3 * 2 * leaves, 128), F32),
            pltpu.VMEM((leaves, rank, leaf), F32),
            pltpu.VMEM((leaves * rank, rank), F32),
            pltpu.VMEM((nodes, rank, rank), F32),
            pltpu.VMEM((FEATS * 2 * leaves, 128), F32),
            pltpu.VMEM((nodes * rank, rank), F32),
            pltpu.SemaphoreType.DMA((6,)),
        ],
        compiler_params=params(),
        name="prepare",
    )(
        cluster_owner,
        in_hbm(vec),
        in_hbm(lanes(leaf_order)),
        in_hbm(lanes(offsets)),
        in_hbm(basis.reshape(leaves, rank, leaf)),
        in_hbm(transfer2),
        in_hbm(top_coupling),
    )

    top = sent[halo_rows:]
    merged = n_row == 4
    if merged:
        got = permute(sent, other_row)
    else:
        got = permute(sent[:halo_rows], odd_rows)
    pair_sib = permute(pair, sibling)
    vec_sib = permute(vec, sibling)

    near_slots = in_hbm(jnp.transpose(near_mask, (1, 2, 0)))
    far_slots = in_hbm(jnp.transpose(far_mask, (1, 2, 0)))
    near_table = pltpu.SMEM((rows, cols, 9), jnp.int32)
    near_shape = jax.ShapeDtypeStruct((leaves, rhs, leaf), F32)
    near, targets, factors = pl.pallas_call(
        functools.partial(own_kernel, rows, cols, rhs, rank, leaf),
        out_shape=(
            near_shape,
            jax.ShapeDtypeStruct((leaves, K, leaf), BF16),
            jax.ShapeDtypeStruct((9, K, 128), BF16),
        ),
        in_specs=[ANY, VMEM, VMEM],
        out_specs=(VMEM,) * 3,
        scratch_shapes=[
            near_table,
            pltpu.VMEM((FEATS * 2 * leaves, 128), F32),
            pltpu.VMEM((leaves, leaf, K), BF16),
            pltpu.VMEM((leaves, 2 * rhs, leaf), BF16),
            pltpu.SemaphoreType.DMA((1,)),
        ],
        compiler_params=params(),
        name="own",
    )(near_slots, vec, pair)

    got, near = lax.optimization_barrier((got, near))
    side_rows = comps * (rows + 2) * 2
    column_rows = side_rows + 3 * rows * rhs
    above, below, coef_mid, even_sent, odd_sent = pl.pallas_call(
        functools.partial(gather_kernel, rows, cols, rhs, n_row),
        out_shape=tuple(
            jax.ShapeDtypeStruct((count, 128), F32)
            for count in (near_rows, near_rows, 3 * coef_rows, column_rows + top_rows, column_rows)
        ),
        in_specs=[ANY] * 4 + [VMEM],
        out_specs=(VMEM,) * 5,
        scratch_shapes=[
            pltpu.VMEM(vec.shape, F32),
            pltpu.VMEM(vec.shape, F32),
            pltpu.VMEM(pair.shape, F32),
            pltpu.VMEM(got.shape, F32),
            pltpu.SemaphoreType.DMA((4,)),
        ],
        compiler_params=params(),
        name="gather",
    )(vec, vec_sib, pair_sib, got, pair)

    if merged:
        top = top + got[halo_rows:]
    top = top + permute(top, sibling)
    even_sent = lax.dynamic_update_slice(even_sent, top, (column_rows, 0))
    got_even = permute(even_sent, even_cols)
    got_odd = permute(odd_sent, odd_cols)

    near = pl.pallas_call(
        functools.partial(rows_kernel, rows, cols, rhs, leaf),
        out_shape=near_shape,
        in_specs=[ANY] + [VMEM] * 5,
        out_specs=VMEM,
        scratch_shapes=[
            near_table,
            pltpu.VMEM((FEATS * 2 * cols, 128), F32),
            pltpu.VMEM((2 * cols, leaf, K), BF16),
            pltpu.VMEM((2 * cols, 2 * rhs, leaf), BF16),
            pltpu.SemaphoreType.DMA((1,)),
        ],
        compiler_params=params(),
        name="rows",
    )(near_slots, above, below, targets, factors, near)

    top, near = lax.optimization_barrier((top + got_even[column_rows:], near))
    left = jnp.where(col_even, got_odd, got_even[:column_rows])
    right = jnp.where(col_even, got_even[:column_rows], got_odd)

    steps = [] if merged else [n_col << k for k in range(1, n_row.bit_length() - 1)]
    steps += [2 << k for k in range(n_col.bit_length() - 2)]
    far = pl.pallas_call(
        functools.partial(far_kernel, rows, cols, rhs, rank, far_offsets()),
        out_shape=near_shape,
        in_specs=[ANY] + [VMEM] * 3 + [ANY, VMEM],
        out_specs=VMEM,
        scratch_shapes=[
            pltpu.SMEM((rows, cols, 16), jnp.int32),
            pltpu.VMEM(coupling.shape, F32),
            pltpu.VMEM(((rows + 4) * (cols + 4), rhs, 2 * rank), F32),
            pltpu.VMEM((2 * leaves * rhs, 16 * rank), BF16),
            pltpu.SemaphoreType.DMA((2,)),
        ],
        compiler_params=params(),
        name="far",
    )(far_slots, left[side_rows:], right[side_rows:], coef_mid, in_hbm(coupling), basis_own)

    top = doubled(top, steps[0])
    top, far, basis_own = lax.optimization_barrier((top, far, basis_own))
    down = pl.pallas_call(
        functools.partial(down_kernel, leaves, rank),
        out_shape=jax.ShapeDtypeStruct((leaves, 2 * rank, leaf), BF16),
        in_specs=[VMEM, VMEM],
        out_specs=VMEM,
        compiler_params=params(),
        name="down",
    )(basis_own, transfer2)

    for step in steps[1:]:
        top = doubled(top, step)

    sides = 2 * (rows + 2)
    base = pl.pallas_call(
        functools.partial(side_kernel, rows, cols, rhs, leaf),
        out_shape=near_shape,
        in_specs=[ANY] + [VMEM] * 6,
        out_specs=VMEM,
        scratch_shapes=[
            near_table,
            pltpu.VMEM((FEATS * sides, 128), F32),
            pltpu.VMEM((sides, leaf, K), BF16),
            pltpu.VMEM((sides, 2 * rhs, leaf), BF16),
            pltpu.SemaphoreType.DMA((1,)),
        ],
        compiler_params=params(),
        name="side",
    )(near_slots, left[:side_rows], right[:side_rows], targets, factors, near, far)

    out = pl.pallas_call(
        functools.partial(finish_kernel, rows, cols, rhs, rank, nodes),
        out_shape=jax.ShapeDtypeStruct((rhs * 2 * leaves, 128), F32),
        in_specs=[VMEM] * 4,
        out_specs=VMEM,
        compiler_params=params(),
        name="finish",
    )(owner, top, down, base)
    out = jnp.swapaxes(out.reshape(rhs, rows, 2, cols, 128), 2, 3)
    return out.reshape(rhs, rows, cols, leaf)


def solution(mesh):
    in_specs = (
        P(None, "row", "col", None),
        P("row", "col", None),
        P(None, "row", "col", None),
        P(None, "row", "col"),
        P(None, "row", "col"),
        P("row", "col", None, None),
        P("row", "col", None, None),
        P(),
        P(),
        P("row", "col"),
    )
    out_specs = P(None, "row", "col", None)
    return jax.shard_map(
        on_device, mesh=mesh, in_specs=in_specs, out_specs=out_specs, check_vma=False
    )
```

```python
import functools

import jax
import jax.numpy as jnp
import numpy as np
from jax import lax
from jax.experimental import pallas as pl
from jax.experimental.pallas import tpu as pltpu
from jax.sharding import PartitionSpec as P

softening = 0.01
F32 = jnp.float32
BF16 = jnp.bfloat16
AXES = ("row", "col")
NT = (((1,), (1,)), ((), ()))
TN = (((0,), (0,)), ((), ()))
NN = (((1,), (0,)), ((), ()))
FEATS = 16
K = 32


def far_offsets():
    found = []
    for down_step in range(-2, 3):
        for right_step in range(-2, 3):
            if max(abs(down_step), abs(right_step)) == 2:
                found.append((down_step, right_step))
    return found


def dot(a, b, dims=NN):
    return lax.dot_general(a, b, dims, preferred_element_type=F32)


def split(x):
    hi = x.astype(BF16)
    lo = (x - hi.astype(F32)).astype(BF16)
    return hi, lo


def dot_parts(a, b_hi, b_lo, dims=NN):
    rows = a.shape[0]
    both = jnp.concatenate(split(a), 0)
    first, second = dot(both, b_hi, dims), dot(both, b_lo, dims)
    return (first[:rows] + first[rows:]) + (second[:rows] + second[rows:])


def dot3(a, b, dims=NN):
    return dot_parts(a, *split(b), dims)


def strided(ref, start, half, count, stride):
    first = ref[pl.ds(start, count, stride=stride), :]
    second = ref[pl.ds(start + half, count, stride=stride), :]
    return jnp.concatenate([first, second], 1)


def put_strided(ref, start, half, count, stride, x):
    ref[pl.ds(start, count, stride=stride), :] = x[:, :128]
    ref[pl.ds(start + half, count, stride=stride), :] = x[:, 128:]


def products(slot):
    step = (slot // 3 - 1, slot % 3 - 1)
    one = 6
    found = []
    for comp in range(3):
        for mine in (comp, 8 + comp):
            for other in (comp, 8 + comp):
                found.append((mine, other, -2.0))
    for part in range(3):
        found.append((3 + part, one, 1.0))
        found.append((one, 3 + part, 1.0))
    for comp in range(2):
        for part in (comp, 8 + comp):
            found.append((part, one, 2.0 * step[comp]))
            found.append((one, part, -2.0 * step[comp]))
    rest = np.float32(softening)
    for _ in range(3):
        part = np.float32(np.asarray(rest, jnp.bfloat16))
        found.append((one, one, float(part)))
        rest = np.float32(rest - part)
    found.append((one, one, float(step[0] ** 2 + step[1] ** 2)))
    return found


def source_choice():
    feat = lax.broadcasted_iota(jnp.int32, (FEATS, K), 0)
    at = lax.broadcasted_iota(jnp.int32, (FEATS, K), 1)
    chosen = jnp.zeros((FEATS, K), F32)
    for i, (mine, _, _) in enumerate(products(0)):
        chosen = jnp.where((at == i) & (feat == mine), 1.0, chosen)
    return chosen.astype(BF16)


def target_choice():
    at = lax.broadcasted_iota(jnp.int32, (K, FEATS), 0)
    feat = lax.broadcasted_iota(jnp.int32, (K, FEATS), 1)
    chosen = jnp.zeros((K, FEATS), F32)
    for i, (_, other, _) in enumerate(products(0)):
        chosen = jnp.where((at == i) & (feat == other), 1.0, chosen)
    return chosen.astype(BF16)


def put_factors(factors):
    at = lax.broadcasted_iota(jnp.int32, (K, 128), 0)
    for slot in range(9):
        factor = jnp.zeros((K, 128), F32)
        for i, (_, _, value) in enumerate(products(slot)):
            if value:
                factor = jnp.where(at == i, value, factor)
        factors[slot] = factor.astype(BF16)


def start_all(pairs, sems):
    copies = [pltpu.make_async_copy(src, dst, sems.at[i]) for i, (src, dst) in enumerate(pairs)]
    for copy in copies:
        copy.start()
    return copies


def prepare_kernel(rows, cols, rhs, rank, leaf, nodes,
                   owner_ref, vec_any, order_any, off_any, basis_any, transfer_any, table_any,
                   pair_ref, basis_out, sent_ref, owner_out,
                   vec, order, off, basis, transfer, table, feat, rolled, sems):
    leaves = rows * cols
    lines = 2 * leaves
    copies = start_all(
        [(order_any, order), (off_any, off), (basis_any, basis), (vec_any, vec), (transfer_any, transfer), (table_any, table)],
        sems,
    )
    copies[0].wait()
    copies[1].wait()
    for comp in range(3):
        u = off[pl.ds(comp * lines, lines), :] - 0.5
        if comp == 2:
            u = u * 0.25
        hi = u.astype(BF16).astype(F32)
        feat[pl.ds(2 * comp * lines, lines), :] = hi
        feat[pl.ds((2 * comp + 1) * lines, lines), :] = (u - hi).astype(BF16).astype(F32)
    feat[pl.ds(6 * lines, 10 * lines), :] = jnp.zeros((10 * lines, 128), F32)
    copies[2].wait()
    copies[3].wait()
    spots = lax.broadcasted_iota(jnp.int32, (leaf, leaf), 0)
    offs = []
    for at in range(leaves):
        start = (at // cols) * 2 * cols + at % cols
        own_order = jnp.concatenate([order[pl.ds(start, 1), :], order[pl.ds(start + cols, 1), :]], 1)
        chosen = (jnp.broadcast_to(own_order, (leaf, leaf)) == spots).astype(F32).astype(BF16)
        bh, bl = split(basis[at])
        own = strided(feat, start, cols, FEATS, lines).astype(BF16)
        moved = dot(jnp.concatenate([bh, bl, own], 0), chosen, NT)
        basis_out[at] = moved[: 2 * rank].astype(BF16)
        offs.append(moved[2 * rank :])
    coefs = []
    for at in range(leaves):
        start = (at // cols) * 2 * cols + at % cols
        xh, xl = split(strided(vec, start, cols, rhs, lines))
        four = dot(jnp.concatenate([xh, xl], 0), basis_out[at], NT)
        coefs.append(four[:rhs, :rank] + four[:rhs, rank:] + four[rhs:, :rank] + four[rhs:, rank:])
    for at in range(leaves):
        start = (at // cols) * 2 * cols + at % cols
        for comp in range(3):
            line = offs[at][2 * comp : 2 * comp + 1] + offs[at][2 * comp + 1 : 2 * comp + 2]
            pair_ref[pl.ds(comp * lines + start, 1), :] = line[:, :128]
            pair_ref[pl.ds(comp * lines + start + cols, 1), :] = line[:, 128:]
    wide = [jnp.concatenate([coefs[2 * p], coefs[2 * p + 1]], 1) for p in range(leaves // 2)]
    row = jnp.where(lax.rem(lax.axis_index("row"), 2) == 0, 0, (rows - 1) * 2 * cols)
    for comp in range(3 + rhs):
        ref, first = (pair_ref, comp) if comp < 3 else (vec, comp - 3)
        sent_ref[pl.ds(comp * 2 * cols, 2 * cols), :] = ref[pl.ds(pl.multiple_of(first * lines + row, 2 * cols), 2 * cols), :]
    near_rows = (3 + rhs) * 2 * cols
    for p in range(leaves // 2):
        pair_ref[pl.ds(3 * lines + p * rhs, rhs), :] = wide[p]
        sent_ref[pl.ds(near_rows + p * rhs, rhs), :] = wide[p]
    copies[4].wait()
    cluster = dot3(jnp.concatenate(wide, 1), transfer[...])
    copies[5].wait()
    owner = owner_ref[0, 0]
    owner_out[...] = jnp.full(owner_out.shape, owner, jnp.int32)
    for node in range(nodes):
        gap = lax.rem(node - owner + nodes, nodes)
        rolled[pl.ds(node * rank, rank), :] = table[gap] * jnp.where(gap == 0, 0.0, 1.0)
    terms = dot3(cluster, rolled[...], NT)
    for pair in range(nodes // 2):
        sent_ref[pl.ds(near_rows + (leaves // 2 + pair) * rhs, rhs), :] = terms[:, pair * 2 * rank : (pair + 1) * 2 * rank]


def fill(into, ref, lines):
    total = jnp.zeros((lines, 128), F32)
    for comp in range(3):
        u = ref[pl.ds(comp * lines, lines), :]
        hi = u.astype(BF16).astype(F32)
        into[pl.ds(comp * lines, lines), :] = hi
        into[pl.ds((8 + comp) * lines, lines), :] = u - hi
        total = total + u * u
    for part in range(3):
        hi = total.astype(BF16).astype(F32)
        into[pl.ds((3 + part) * lines, lines), :] = hi
        total = total - hi
    into[pl.ds(6 * lines, lines), :] = jnp.ones((lines, 128), F32)
    for unused in (7, 11, 12, 13, 14, 15):
        into[pl.ds(unused * lines, lines), :] = jnp.zeros((lines, 128), F32)


def leaf_features(ref, start, half, stride):
    u = strided(ref, start, half, 8, stride)
    row = lax.broadcasted_iota(jnp.int32, u.shape, 0)
    u = jnp.where(row < 3, u, 0.0)
    hi = u.astype(BF16).astype(F32)
    first = hi
    total = jnp.sum(u * u, axis=0, keepdims=True)
    for part in range(3):
        square = total.astype(BF16).astype(F32)
        first = jnp.where(row == 3 + part, square, first)
        total = total - square
    first = jnp.where(row == 6, 1.0, first)
    return jnp.concatenate([first, u - hi], 0).astype(BF16)


def step_target(targets, factors, at, slot):
    factor = factors[slot]
    return targets[at] * jnp.concatenate([factor, factor], 1)


def place(points, spread, values, source_map, rhs, start, half, stride, at):
    spread[at] = dot(leaf_features(points, start, half, stride), source_map, TN).astype(BF16)
    xh, xl = split(strided(points, 3 * stride + start, half, rhs, stride))
    values[at] = jnp.concatenate([xh, xl], 0)


def tile_product(spread, target, values, keep):
    kh, kl = split(lax.rsqrt(dot(spread, target)))
    x = jnp.where(keep, values, jnp.zeros_like(values))
    rhs = x.shape[0] // 2
    first, second = dot(x, kh), dot(x, kl)
    return (first[:rhs] + first[rhs:]) + (second[:rhs] + second[rhs:])


def own_kernel(rows, cols, rhs, rank, leaf,
               mask_any, vec, pos_ref,
               near_ref, targets, factors,
               near_mask, feat, spread, values, sems):
    copies = start_all([(mask_any, near_mask)], sems)
    leaves = rows * cols
    lines = 2 * leaves
    fill(feat, pos_ref, lines)
    put_factors(factors)
    source_map, target_map = source_choice(), target_choice()
    for at in range(leaves):
        start = (at // cols) * 2 * cols + at % cols
        own = strided(feat, start, cols, FEATS, lines).astype(BF16)
        spread[at] = dot(own, source_map, TN).astype(BF16)
    for at in range(leaves):
        start = (at // cols) * 2 * cols + at % cols
        own = strided(feat, start, cols, FEATS, lines).astype(BF16)
        targets[at] = dot(target_map, own).astype(BF16)
    for at in range(leaves):
        start = (at // cols) * 2 * cols + at % cols
        xh, xl = split(strided(vec, start, cols, rhs, lines))
        values[at] = jnp.concatenate([xh, xl], 0)
    copies[0].wait()
    for at in range(leaves):
        row, col = at // cols, at % cols
        total = jnp.zeros((rhs, leaf), F32)
        for slot in range(9):
            to_row, to_col = row + slot // 3 - 1, col + slot % 3 - 1
            if 0 <= to_row < rows and 0 <= to_col < cols:
                other = to_row * cols + to_col
                total = total + tile_product(
                    spread[other], step_target(targets, factors, at, slot), values[other], near_mask[row, col, slot] != 0
                )
        near_ref[at] = total


def down_kernel(leaves, rank, basis_ref, transfer, down_ref):
    for at in range(leaves):
        both = basis_ref[at]
        th, tl = split(transfer[pl.ds(at * rank, rank), :])
        moved = dot(th, both[:rank], TN) + dot(tl, both[:rank], TN) + dot(th, both[rank:], TN)
        gh, gl = split(moved)
        down_ref[at] = jnp.concatenate([gh, gl], 0)


def gather_kernel(rows, cols, rhs, n_row,
                  vec_any, vec_sib_any, pair_sib_any, got_any, pair,
                  above_ref, below_ref, coef_ref, even_ref, odd_ref,
                  vec, vec_sib, pair_sib, got, sems):
    copies = start_all(
        [(vec_any, vec), (vec_sib_any, vec_sib), (pair_sib_any, pair_sib), (got_any, got)], sems
    )
    comps = 3 + rhs
    lines = 2 * rows * cols
    line = 2 * cols
    my_row = lax.axis_index("row")
    row_even = lax.rem(my_row, 2) == 0
    col_even = lax.rem(lax.axis_index("col"), 2) == 0
    beyond = jnp.where(row_even, my_row > 0, my_row < n_row - 1)
    for copy in copies:
        copy.wait()
    row = jnp.where(row_even, 0, (rows - 1) * line)
    for comp in range(comps):
        ref, first = (pair_sib, comp) if comp < 3 else (vec_sib, comp - 3)
        near = ref[pl.ds(pl.multiple_of(first * lines + row, line), line), :]
        mine = pl.ds(comp * line, line)
        far = jnp.where(beyond, got[mine, :], 0.0)
        above_ref[mine, :] = jnp.where(row_even, far, near)
        below_ref[mine, :] = jnp.where(row_even, near, far)
    block = rows * cols // 2 * rhs
    own_coef = pl.ds(3 * lines, block)
    near = pair_sib[own_coef, :]
    far = jnp.where(beyond, got[pl.ds(comps * line, block), :], 0.0)
    coef_ref[pl.ds(0, block), :] = jnp.where(row_even, far, near)
    coef_ref[pl.ds(block, block), :] = pair[own_coef, :]
    coef_ref[pl.ds(2 * block, block), :] = jnp.where(row_even, near, far)

    def send(low, high, start, count, stride):
        where = pl.ds(start, count) if stride == 1 else pl.ds(start, count, stride=stride)
        even_ref[where, :] = jnp.where(col_even, high, low)
        odd_ref[where, :] = jnp.where(col_even, low, high)

    def column(ref, start, count, stride):
        return [ref[pl.ds(start + at, count, stride=stride), :] for at in (0, cols - 1)]

    side = 2 * (rows + 2)
    for half in range(2):
        send(*column(above_ref, half * cols, comps, line), half, comps, side)
        send(*column(below_ref, half * cols, comps, line), 2 * (rows + 1) + half, comps, side)
        for r in range(rows):
            to = 2 * (r + 1) + half
            send(*column(pair, (2 * r + half) * cols, 3, lines), to, 3, side)
            send(*column(vec, (2 * r + half) * cols, rhs, lines), 3 * side + to, rhs, side)
    pairs = cols // 2
    for at in range(3 * rows):
        low = coef_ref[pl.ds(at * pairs * rhs, rhs), :]
        high = coef_ref[pl.ds((at * pairs + pairs - 1) * rhs, rhs), :]
        send(low, high, comps * side + at * rhs, rhs, 1)


def rows_kernel(rows, cols, rhs, leaf,
                mask_any, above_ref, below_ref, targets, factors, near_in,
                near_ref,
                near_mask, spread, values, sems):
    copies = start_all([(mask_any, near_mask)], sems)
    source_map = source_choice()
    for ref, line in ((above_ref, 0), (below_ref, 1)):
        for col in range(cols):
            place(ref, spread, values, source_map, rhs, col, cols, 2 * cols, line * cols + col)
    copies[0].wait()
    for at in range(rows * cols):
        row, col = at // cols, at % cols
        total = near_in[at]
        for slot in range(9):
            to_row, to_col = row + slot // 3 - 1, col + slot % 3 - 1
            if not 0 <= to_row < rows and 0 <= to_col < cols:
                other = (0 if to_row < 0 else cols) + to_col
                total = total + tile_product(
                    spread[other], step_target(targets, factors, at, slot), values[other], near_mask[row, col, slot] != 0
                )
        near_ref[at] = total


def far_kernel(rows, cols, rhs, rank, far_list,
               far_any, left_ref, right_ref, coef_ref, coupling, basis_ref,
               far_ref,
               far_mask, dup, wide, sems):
    copies = start_all([(far_any, far_mask)], sems)
    leaves = rows * cols
    low = lax.broadcasted_iota(jnp.int32, (rhs, 2 * rank), 1) < rank
    pairs = cols // 2
    for line in range(rows + 4):
        for pair in range(pairs + 2):
            if pair == 0:
                both = left_ref[pl.ds(line * rhs, rhs), :]
            elif pair == pairs + 1:
                both = right_ref[pl.ds(line * rhs, rhs), :]
            else:
                both = coef_ref[pl.ds((line * pairs + pair - 1) * rhs, rhs), :]
            turned = pltpu.roll(both, rank, 1)
            at = line * (cols + 4) + 2 * pair
            dup[at] = jnp.where(low, both, turned)
            dup[at + 1] = jnp.where(low, turned, both)
    copies[0].wait()
    for row in range(rows):
        for col in range(cols):
            at = row * cols + col
            for chunk in range(len(far_list) // 2):
                parts = []
                for slot in (2 * chunk, 2 * chunk + 1):
                    down_step, right_step = far_list[slot]
                    part = dup[(row + 2 + down_step) * (cols + 4) + col + 2 + right_step]
                    parts.append(jnp.where(far_mask[row, col, slot] != 0, part, 0.0))
                hi, lo = split(jnp.where(low, parts[0], parts[1]))
                wide[pl.ds(at * rhs, rhs), pl.ds(chunk * 2 * rank, 2 * rank)] = hi
                wide[pl.ds((leaves + at) * rhs, rhs), pl.ds(chunk * 2 * rank, 2 * rank)] = lo
    both = jnp.concatenate(split(jnp.concatenate([coupling[slot] for slot in range(len(far_list))], 1)), 0)
    four = dot(wide[...], both, NT)
    half = leaves * rhs
    far = (four[:half, :rank] + four[half:, :rank]) + (four[:half, rank:] + four[half:, rank:])
    for at in range(leaves):
        both = basis_ref[at]
        far_ref[at] = dot_parts(far[at * rhs : (at + 1) * rhs], both[:rank], both[rank:])


def side_kernel(rows, cols, rhs, leaf,
                mask_any, left_ref, right_ref, targets, factors, near_ref, far_ref,
                base_ref,
                near_mask, spread, values, sems):
    copies = start_all([(mask_any, near_mask)], sems)
    source_map = source_choice()
    side = 2 * (rows + 2)
    for ref, first in ((left_ref, 0), (right_ref, rows + 2)):
        for line in range(rows + 2):
            place(ref, spread, values, source_map, rhs, 2 * line, 1, side, first + line)
    copies[0].wait()
    scale = 1.0 / (3.0 * float(leaf) ** 0.5)
    for at in range(rows * cols):
        row, col = at // cols, at % cols
        total = near_ref[at]
        for slot in range(9):
            to_row, to_col = row + slot // 3 - 1, col + slot % 3 - 1
            if not 0 <= to_col < cols:
                other = (0 if to_col < 0 else rows + 2) + to_row + 1
                total = total + tile_product(
                    spread[other], step_target(targets, factors, at, slot), values[other], near_mask[row, col, slot] != 0
                )
        base_ref[at] = total * scale + far_ref[at]


def finish_kernel(rows, cols, rhs, rank, nodes, owner_ref, top_ref, down_ref, base_ref, out_ref):
    lines = 2 * rows * cols
    high = (lax.broadcasted_iota(jnp.int32, (rhs, 2 * rank), 1) >= rank).astype(jnp.int32)
    owner = owner_ref[...] - high
    chosen = jnp.zeros((rhs, 2 * rank), F32)
    for pair in range(nodes // 2):
        chosen = jnp.where(owner == 2 * pair, top_ref[pl.ds(pair * rhs, rhs), :], chosen)
    local = (chosen + pltpu.roll(chosen, rank, 1))[:, :rank]
    for at in range(rows * cols):
        down = dot_parts(local, down_ref[at, pl.ds(0, rank)], down_ref[at, pl.ds(rank, rank)])
        start = (at // cols) * 2 * cols + at % cols
        put_strided(out_ref, start, cols, rhs, lines, base_ref[at] + down)


VMEM = pl.BlockSpec(memory_space=pltpu.VMEM)
SMEM = pl.BlockSpec(memory_space=pltpu.SMEM)
ANY = pl.BlockSpec(memory_space=pltpu.HBM)


def lanes(x):
    x = x.reshape(x.shape[:-1] + (2, 128))
    return jnp.swapaxes(x, -3, -2).reshape(-1, 128)


def on_device(
    vectors,
    leaf_order,
    offsets,
    near_mask,
    far_mask,
    basis,
    transfer,
    coupling,
    top_coupling,
    cluster_owner,
):
    rhs, rows, cols, leaf = vectors.shape
    rank = basis.shape[2]
    nodes = top_coupling.shape[0]
    leaves = rows * cols
    n_row, n_col = lax.axis_size("row"), lax.axis_size("col")
    devices = n_row * n_col
    col_even = lax.axis_index("col") % 2 == 0
    comps = 3 + rhs
    near_rows = comps * 2 * cols
    coef_rows = leaves // 2 * rhs
    top_rows = nodes // 2 * rhs
    halo_rows = near_rows + coef_rows

    def params():
        return pltpu.CompilerParams(vmem_limit_bytes=12 * 1024 * 1024)

    def grid_perm(step):
        return [
            (r * n_col + c, t[0] * n_col + t[1])
            for r in range(n_row)
            for c in range(n_col)
            for t in [step(r, c)]
            if t is not None
        ]

    def permute(x, step):
        return lax.ppermute(x, AXES, grid_perm(step))

    def sibling(r, c):
        return (r ^ 1, c)

    def odd_rows(r, c):
        t = r + 1 if r % 2 else r - 1
        return (t, c) if 0 <= t < n_row else None

    def other_row(r, c):
        return (n_row - 1 - r, c)

    def even_cols(r, c):
        return (r, c ^ 1)

    def odd_cols(r, c):
        t = c + 1 if c % 2 else c - 1
        return (r, t) if 0 <= t < n_col else None

    def doubled(x, step):
        return x + lax.ppermute(x, AXES, [(i, i ^ step) for i in range(devices)])

    def in_hbm(x):
        return pltpu.with_memory_space_constraint(x, pltpu.HBM)

    vec = lanes(vectors)
    transfer2 = transfer.reshape(leaves * rank, rank)
    pair, basis_own, sent, owner = pl.pallas_call(
        functools.partial(prepare_kernel, rows, cols, rhs, rank, leaf, nodes),
        out_shape=(
            jax.ShapeDtypeStruct((3 * 2 * leaves + coef_rows, 128), F32),
            jax.ShapeDtypeStruct((leaves, 2 * rank, leaf), BF16),
            jax.ShapeDtypeStruct((halo_rows + top_rows, 128), F32),
            jax.ShapeDtypeStruct((rhs, 2 * rank), jnp.int32),
        ),
        in_specs=[SMEM] + [ANY] * 6,
        out_specs=(VMEM,) * 4,
        scratch_shapes=[
            pltpu.VMEM((rhs * 2 * leaves, 128), F32),
            pltpu.VMEM((2 * leaves, 128), jnp.int32),
            pltpu.VMEM((3 * 2 * leaves, 128), F32),
            pltpu.VMEM((leaves, rank, leaf), F32),
            pltpu.VMEM((leaves * rank, rank), F32),
            pltpu.VMEM((nodes, rank, rank), F32),
            pltpu.VMEM((FEATS * 2 * leaves, 128), F32),
            pltpu.VMEM((nodes * rank, rank), F32),
            pltpu.SemaphoreType.DMA((6,)),
        ],
        compiler_params=params(),
        name="prepare",
    )(
        cluster_owner,
        in_hbm(vec),
        in_hbm(lanes(leaf_order)),
        in_hbm(lanes(offsets)),
        in_hbm(basis.reshape(leaves, rank, leaf)),
        in_hbm(transfer2),
        in_hbm(top_coupling),
    )

    top = sent[halo_rows:]
    merged = n_row == 4
    if merged:
        got = permute(sent, other_row)
    else:
        got = permute(sent[:halo_rows], odd_rows)
    pair_sib = permute(pair, sibling)
    vec_sib = permute(vec, sibling)

    near_slots = in_hbm(jnp.transpose(near_mask, (1, 2, 0)))
    far_slots = in_hbm(jnp.transpose(far_mask, (1, 2, 0)))
    near_table = pltpu.SMEM((rows, cols, 9), jnp.int32)
    near_shape = jax.ShapeDtypeStruct((leaves, rhs, leaf), F32)
    near, targets, factors = pl.pallas_call(
        functools.partial(own_kernel, rows, cols, rhs, rank, leaf),
        out_shape=(
            near_shape,
            jax.ShapeDtypeStruct((leaves, K, leaf), BF16),
            jax.ShapeDtypeStruct((9, K, 128), BF16),
        ),
        in_specs=[ANY, VMEM, VMEM],
        out_specs=(VMEM,) * 3,
        scratch_shapes=[
            near_table,
            pltpu.VMEM((FEATS * 2 * leaves, 128), F32),
            pltpu.VMEM((leaves, leaf, K), BF16),
            pltpu.VMEM((leaves, 2 * rhs, leaf), BF16),
            pltpu.SemaphoreType.DMA((1,)),
        ],
        compiler_params=params(),
        name="own",
    )(near_slots, vec, pair)

    got, near = lax.optimization_barrier((got, near))
    side_rows = comps * (rows + 2) * 2
    column_rows = side_rows + 3 * rows * rhs
    above, below, coef_mid, even_sent, odd_sent = pl.pallas_call(
        functools.partial(gather_kernel, rows, cols, rhs, n_row),
        out_shape=tuple(
            jax.ShapeDtypeStruct((count, 128), F32)
            for count in (near_rows, near_rows, 3 * coef_rows, column_rows + top_rows // 2, column_rows)
        ),
        in_specs=[ANY] * 4 + [VMEM],
        out_specs=(VMEM,) * 5,
        scratch_shapes=[
            pltpu.VMEM(vec.shape, F32),
            pltpu.VMEM(vec.shape, F32),
            pltpu.VMEM(pair.shape, F32),
            pltpu.VMEM(got.shape, F32),
            pltpu.SemaphoreType.DMA((4,)),
        ],
        compiler_params=params(),
        name="gather",
    )(vec, vec_sib, pair_sib, got, pair)

    if merged:
        top = top + got[halo_rows:]
    half = top_rows // 2
    row_even = lax.axis_index("row") % 2 == 0
    kept = permute(jnp.where(row_even, top[half:], top[:half]), sibling)
    top = jnp.where(row_even, top[:half], top[half:]) + kept
    even_sent = lax.dynamic_update_slice(even_sent, top, (column_rows, 0))
    got_even = permute(even_sent, even_cols)
    got_odd = permute(odd_sent, odd_cols)

    near = pl.pallas_call(
        functools.partial(rows_kernel, rows, cols, rhs, leaf),
        out_shape=near_shape,
        in_specs=[ANY] + [VMEM] * 5,
        out_specs=VMEM,
        scratch_shapes=[
            near_table,
            pltpu.VMEM((2 * cols, leaf, K), BF16),
            pltpu.VMEM((2 * cols, 2 * rhs, leaf), BF16),
            pltpu.SemaphoreType.DMA((1,)),
        ],
        compiler_params=params(),
        name="rows",
    )(near_slots, above, below, targets, factors, near)

    top, near = lax.optimization_barrier((top + got_even[column_rows:], near))
    left = jnp.where(col_even, got_odd, got_even[:column_rows])
    right = jnp.where(col_even, got_even[:column_rows], got_odd)

    steps = [] if merged else [n_col << k for k in range(1, n_row.bit_length() - 1)]
    steps += [2 << k for k in range(n_col.bit_length() - 2)]
    far = pl.pallas_call(
        functools.partial(far_kernel, rows, cols, rhs, rank, far_offsets()),
        out_shape=near_shape,
        in_specs=[ANY] + [VMEM] * 5,
        out_specs=VMEM,
        scratch_shapes=[
            pltpu.SMEM((rows, cols, 16), jnp.int32),
            pltpu.VMEM(((rows + 4) * (cols + 4), rhs, 2 * rank), F32),
            pltpu.VMEM((2 * leaves * rhs, 16 * rank), BF16),
            pltpu.SemaphoreType.DMA((1,)),
        ],
        compiler_params=params(),
        name="far",
    )(far_slots, left[side_rows:], right[side_rows:], coef_mid, coupling, basis_own)

    top = doubled(top, steps[0])
    top, far, basis_own = lax.optimization_barrier((top, far, basis_own))
    down = pl.pallas_call(
        functools.partial(down_kernel, leaves, rank),
        out_shape=jax.ShapeDtypeStruct((leaves, 2 * rank, leaf), BF16),
        in_specs=[VMEM, VMEM],
        out_specs=VMEM,
        compiler_params=params(),
        name="down",
    )(basis_own, transfer2)

    for step in steps[1:]:
        top = doubled(top, step)

    sides = 2 * (rows + 2)
    base = pl.pallas_call(
        functools.partial(side_kernel, rows, cols, rhs, leaf),
        out_shape=near_shape,
        in_specs=[ANY] + [VMEM] * 6,
        out_specs=VMEM,
        scratch_shapes=[
            near_table,
            pltpu.VMEM((sides, leaf, K), BF16),
            pltpu.VMEM((sides, 2 * rhs, leaf), BF16),
            pltpu.SemaphoreType.DMA((1,)),
        ],
        compiler_params=params(),
        name="side",
    )(near_slots, left[:side_rows], right[:side_rows], targets, factors, near, far)

    top, base = lax.optimization_barrier((top, base))
    other = permute(top, sibling)
    other, down = lax.optimization_barrier((other, down))
    top = jnp.concatenate([jnp.where(row_even, top, other), jnp.where(row_even, other, top)], 0)
    out = pl.pallas_call(
        functools.partial(finish_kernel, rows, cols, rhs, rank, nodes),
        out_shape=jax.ShapeDtypeStruct((rhs * 2 * leaves, 128), F32),
        in_specs=[VMEM] * 4,
        out_specs=VMEM,
        compiler_params=params(),
        name="finish",
    )(owner, top, down, base)
    out = jnp.swapaxes(out.reshape(rhs, rows, 2, cols, 128), 2, 3)
    return out.reshape(rhs, rows, cols, leaf)


def solution(mesh):
    in_specs = (
        P(None, "row", "col", None),
        P("row", "col", None),
        P(None, "row", "col", None),
        P(None, "row", "col"),
        P(None, "row", "col"),
        P("row", "col", None, None),
        P("row", "col", None, None),
        P(),
        P(),
        P("row", "col"),
    )
    out_specs = P(None, "row", "col", None)
    return jax.shard_map(
        on_device, mesh=mesh, in_specs=in_specs, out_specs=out_specs, check_vma=False
    )
```

```python
import functools

import jax
import jax.numpy as jnp
import numpy as np
from jax import lax
from jax.experimental import pallas as pl
from jax.experimental.pallas import tpu as pltpu
from jax.sharding import PartitionSpec as P

softening = 0.01
F32 = jnp.float32
BF16 = jnp.bfloat16
AXES = ("row", "col")
NT = (((1,), (1,)), ((), ()))
TN = (((0,), (0,)), ((), ()))
NN = (((1,), (0,)), ((), ()))
FEATS = 16
K = 32


def far_offsets():
    found = []
    for down_step in range(-2, 3):
        for right_step in range(-2, 3):
            if max(abs(down_step), abs(right_step)) == 2:
                found.append((down_step, right_step))
    return found


def dot(a, b, dims=NN):
    return lax.dot_general(a, b, dims, preferred_element_type=F32)


def split(x):
    hi = x.astype(BF16)
    lo = (x - hi.astype(F32)).astype(BF16)
    return hi, lo


def dot_parts(a, b_hi, b_lo, dims=NN):
    rows = a.shape[0]
    both = jnp.concatenate(split(a), 0)
    first, second = dot(both, b_hi, dims), dot(both, b_lo, dims)
    return (first[:rows] + first[rows:]) + (second[:rows] + second[rows:])


def dot3(a, b, dims=NN):
    return dot_parts(a, *split(b), dims)


def strided(ref, start, half, count, stride):
    first = ref[pl.ds(start, count, stride=stride), :]
    second = ref[pl.ds(start + half, count, stride=stride), :]
    return jnp.concatenate([first, second], 1)


def put_strided(ref, start, half, count, stride, x):
    ref[pl.ds(start, count, stride=stride), :] = x[:, :128]
    ref[pl.ds(start + half, count, stride=stride), :] = x[:, 128:]


def products(slot):
    step = (slot // 3 - 1, slot % 3 - 1)
    one = 6
    found = []
    for comp in range(3):
        for mine in (comp, 8 + comp):
            for other in (comp, 8 + comp):
                found.append((mine, other, -2.0))
    for part in range(3):
        found.append((3 + part, one, 1.0))
        found.append((one, 3 + part, 1.0))
    for comp in range(2):
        for part in (comp, 8 + comp):
            found.append((part, one, 2.0 * step[comp]))
            found.append((one, part, -2.0 * step[comp]))
    rest = np.float32(softening)
    for _ in range(3):
        part = np.float32(np.asarray(rest, jnp.bfloat16))
        found.append((one, one, float(part)))
        rest = np.float32(rest - part)
    found.append((one, one, float(step[0] ** 2 + step[1] ** 2)))
    return found


def source_choice():
    feat = lax.broadcasted_iota(jnp.int32, (FEATS, K), 0)
    at = lax.broadcasted_iota(jnp.int32, (FEATS, K), 1)
    chosen = jnp.zeros((FEATS, K), F32)
    for i, (mine, _, _) in enumerate(products(0)):
        chosen = jnp.where((at == i) & (feat == mine), 1.0, chosen)
    return chosen.astype(BF16)


def target_choice():
    at = lax.broadcasted_iota(jnp.int32, (K, FEATS), 0)
    feat = lax.broadcasted_iota(jnp.int32, (K, FEATS), 1)
    chosen = jnp.zeros((K, FEATS), F32)
    for i, (_, other, _) in enumerate(products(0)):
        chosen = jnp.where((at == i) & (feat == other), 1.0, chosen)
    return chosen.astype(BF16)


def put_factors(factors):
    at = lax.broadcasted_iota(jnp.int32, (K, 128), 0)
    for slot in range(9):
        factor = jnp.zeros((K, 128), F32)
        for i, (_, _, value) in enumerate(products(slot)):
            if value:
                factor = jnp.where(at == i, value, factor)
        factors[slot] = factor.astype(BF16)


def start_all(pairs, sems):
    copies = [pltpu.make_async_copy(src, dst, sems.at[i]) for i, (src, dst) in enumerate(pairs)]
    for copy in copies:
        copy.start()
    return copies


def prepare_kernel(rows, cols, rhs, rank, leaf, nodes,
                   owner_ref, vec_any, order_any, off_any, basis_any, transfer_any, table_any,
                   pair_ref, basis_out, sent_ref, owner_out,
                   vec, order, off, basis, transfer, table, feat, rolled, sems):
    leaves = rows * cols
    lines = 2 * leaves
    copies = start_all(
        [(order_any, order), (off_any, off), (basis_any, basis), (vec_any, vec), (transfer_any, transfer), (table_any, table)],
        sems,
    )
    copies[0].wait()
    copies[1].wait()
    for comp in range(3):
        u = off[pl.ds(comp * lines, lines), :] - 0.5
        if comp == 2:
            u = u * 0.25
        hi = u.astype(BF16).astype(F32)
        feat[pl.ds(2 * comp * lines, lines), :] = hi
        feat[pl.ds((2 * comp + 1) * lines, lines), :] = (u - hi).astype(BF16).astype(F32)
    feat[pl.ds(6 * lines, 10 * lines), :] = jnp.zeros((10 * lines, 128), F32)
    copies[2].wait()
    copies[3].wait()
    spots = lax.broadcasted_iota(jnp.int32, (leaf, leaf), 0)
    offs = []
    for at in range(leaves):
        start = (at // cols) * 2 * cols + at % cols
        own_order = jnp.concatenate([order[pl.ds(start, 1), :], order[pl.ds(start + cols, 1), :]], 1)
        chosen = (jnp.broadcast_to(own_order, (leaf, leaf)) == spots).astype(F32).astype(BF16)
        bh, bl = split(basis[at])
        own = strided(feat, start, cols, FEATS, lines).astype(BF16)
        moved = dot(jnp.concatenate([bh, bl, own], 0), chosen, NT)
        basis_out[at] = moved[: 2 * rank].astype(BF16)
        offs.append(moved[2 * rank :])
    coefs = []
    for at in range(leaves):
        start = (at // cols) * 2 * cols + at % cols
        xh, xl = split(strided(vec, start, cols, rhs, lines))
        four = dot(jnp.concatenate([xh, xl], 0), basis_out[at], NT)
        coefs.append(four[:rhs, :rank] + four[:rhs, rank:] + four[rhs:, :rank] + four[rhs:, rank:])
    for at in range(leaves):
        start = (at // cols) * 2 * cols + at % cols
        for comp in range(3):
            line = offs[at][2 * comp : 2 * comp + 1] + offs[at][2 * comp + 1 : 2 * comp + 2]
            pair_ref[pl.ds(comp * lines + start, 1), :] = line[:, :128]
            pair_ref[pl.ds(comp * lines + start + cols, 1), :] = line[:, 128:]
    wide = [jnp.concatenate([coefs[2 * p], coefs[2 * p + 1]], 1) for p in range(leaves // 2)]
    row = jnp.where(lax.rem(lax.axis_index("row"), 2) == 0, 0, (rows - 1) * 2 * cols)
    for comp in range(3 + rhs):
        ref, first = (pair_ref, comp) if comp < 3 else (vec, comp - 3)
        sent_ref[pl.ds(comp * 2 * cols, 2 * cols), :] = ref[pl.ds(pl.multiple_of(first * lines + row, 2 * cols), 2 * cols), :]
    near_rows = (3 + rhs) * 2 * cols
    for p in range(leaves // 2):
        pair_ref[pl.ds(3 * lines + p * rhs, rhs), :] = wide[p]
        sent_ref[pl.ds(near_rows + p * rhs, rhs), :] = wide[p]
    copies[4].wait()
    cluster = dot3(jnp.concatenate(wide, 1), transfer[...])
    copies[5].wait()
    owner = owner_ref[0, 0]
    owner_out[...] = jnp.full(owner_out.shape, owner, jnp.int32)
    for node in range(nodes):
        gap = lax.rem(node - owner + nodes, nodes)
        rolled[pl.ds(node * rank, rank), :] = table[gap] * jnp.where(gap == 0, 0.0, 1.0)
    terms = dot3(cluster, rolled[...], NT)
    for pair in range(nodes // 2):
        sent_ref[pl.ds(near_rows + (leaves // 2 + pair) * rhs, rhs), :] = terms[:, pair * 2 * rank : (pair + 1) * 2 * rank]


def fill(into, ref, lines):
    total = jnp.zeros((lines, 128), F32)
    for comp in range(3):
        u = ref[pl.ds(comp * lines, lines), :]
        hi = u.astype(BF16).astype(F32)
        into[pl.ds(comp * lines, lines), :] = hi
        into[pl.ds((8 + comp) * lines, lines), :] = u - hi
        total = total + u * u
    for part in range(3):
        hi = total.astype(BF16).astype(F32)
        into[pl.ds((3 + part) * lines, lines), :] = hi
        total = total - hi
    into[pl.ds(6 * lines, lines), :] = jnp.ones((lines, 128), F32)
    for unused in (7, 11, 12, 13, 14, 15):
        into[pl.ds(unused * lines, lines), :] = jnp.zeros((lines, 128), F32)


def leaf_features(ref, start, half, stride):
    u = strided(ref, start, half, 8, stride)
    row = lax.broadcasted_iota(jnp.int32, u.shape, 0)
    u = jnp.where(row < 3, u, 0.0)
    hi = u.astype(BF16).astype(F32)
    first = hi
    total = jnp.sum(u * u, axis=0, keepdims=True)
    for part in range(3):
        square = total.astype(BF16).astype(F32)
        first = jnp.where(row == 3 + part, square, first)
        total = total - square
    first = jnp.where(row == 6, 1.0, first)
    return jnp.concatenate([first, u - hi], 0).astype(BF16)


def step_target(targets, factors, at, slot):
    factor = factors[slot]
    return targets[at] * jnp.concatenate([factor, factor], 1)


def place(points, spread, values, source_map, rhs, start, half, stride, at):
    spread[at] = dot(leaf_features(points, start, half, stride), source_map, TN).astype(BF16)
    xh, xl = split(strided(points, 3 * stride + start, half, rhs, stride))
    values[at] = jnp.concatenate([xh, xl], 0)


def tile_product(spread, target, values, keep):
    kh, kl = split(lax.rsqrt(dot(spread, target)))
    x = jnp.where(keep, values, jnp.zeros_like(values))
    rhs = x.shape[0] // 2
    first, second = dot(x, kh), dot(x, kl)
    return (first[:rhs] + first[rhs:]) + (second[:rhs] + second[rhs:])


def own_kernel(rows, cols, rhs, rank, leaf,
               mask_any, vec, pos_ref,
               near_ref, targets, factors,
               near_mask, feat, spread, values, sems):
    copies = start_all([(mask_any, near_mask)], sems)
    leaves = rows * cols
    lines = 2 * leaves
    fill(feat, pos_ref, lines)
    put_factors(factors)
    source_map, target_map = source_choice(), target_choice()
    for at in range(leaves):
        start = (at // cols) * 2 * cols + at % cols
        own = strided(feat, start, cols, FEATS, lines).astype(BF16)
        spread[at] = dot(own, source_map, TN).astype(BF16)
    for at in range(leaves):
        start = (at // cols) * 2 * cols + at % cols
        own = strided(feat, start, cols, FEATS, lines).astype(BF16)
        targets[at] = dot(target_map, own).astype(BF16)
    for at in range(leaves):
        start = (at // cols) * 2 * cols + at % cols
        xh, xl = split(strided(vec, start, cols, rhs, lines))
        values[at] = jnp.concatenate([xh, xl], 0)
    copies[0].wait()
    for at in range(leaves):
        row, col = at // cols, at % cols
        total = jnp.zeros((rhs, leaf), F32)
        for slot in range(9):
            to_row, to_col = row + slot // 3 - 1, col + slot % 3 - 1
            if 0 <= to_row < rows and 0 <= to_col < cols:
                other = to_row * cols + to_col
                total = total + tile_product(
                    spread[other], step_target(targets, factors, at, slot), values[other], near_mask[row, col, slot] != 0
                )
        near_ref[at] = total


def down_kernel(leaves, rank, basis_ref, transfer, down_ref):
    for at in range(leaves):
        both = basis_ref[at]
        th, tl = split(transfer[pl.ds(at * rank, rank), :])
        moved = dot(th, both[:rank], TN) + dot(tl, both[:rank], TN) + dot(th, both[rank:], TN)
        gh, gl = split(moved)
        down_ref[at] = jnp.concatenate([gh, gl], 0)


def gather_kernel(rows, cols, rhs, n_row,
                  vec_any, vec_sib_any, pair_sib_any, got_any, pair,
                  above_ref, below_ref, coef_ref, even_ref, odd_ref,
                  vec, vec_sib, pair_sib, got, sems):
    copies = start_all(
        [(vec_any, vec), (vec_sib_any, vec_sib), (pair_sib_any, pair_sib), (got_any, got)], sems
    )
    comps = 3 + rhs
    lines = 2 * rows * cols
    line = 2 * cols
    my_row = lax.axis_index("row")
    row_even = lax.rem(my_row, 2) == 0
    col_even = lax.rem(lax.axis_index("col"), 2) == 0
    beyond = jnp.where(row_even, my_row > 0, my_row < n_row - 1)
    for copy in copies:
        copy.wait()
    row = jnp.where(row_even, 0, (rows - 1) * line)
    for comp in range(comps):
        ref, first = (pair_sib, comp) if comp < 3 else (vec_sib, comp - 3)
        near = ref[pl.ds(pl.multiple_of(first * lines + row, line), line), :]
        mine = pl.ds(comp * line, line)
        far = jnp.where(beyond, got[mine, :], 0.0)
        above_ref[mine, :] = jnp.where(row_even, far, near)
        below_ref[mine, :] = jnp.where(row_even, near, far)
    block = rows * cols // 2 * rhs
    own_coef = pl.ds(3 * lines, block)
    near = pair_sib[own_coef, :]
    far = jnp.where(beyond, got[pl.ds(comps * line, block), :], 0.0)
    coef_ref[pl.ds(0, block), :] = jnp.where(row_even, far, near)
    coef_ref[pl.ds(block, block), :] = pair[own_coef, :]
    coef_ref[pl.ds(2 * block, block), :] = jnp.where(row_even, near, far)

    def send(low, high, start, count, stride):
        where = pl.ds(start, count) if stride == 1 else pl.ds(start, count, stride=stride)
        even_ref[where, :] = jnp.where(col_even, high, low)
        odd_ref[where, :] = jnp.where(col_even, low, high)

    def column(ref, start, count, stride):
        return [ref[pl.ds(start + at, count, stride=stride), :] for at in (0, cols - 1)]

    side = 2 * (rows + 2)
    for half in range(2):
        send(*column(above_ref, half * cols, comps, line), half, comps, side)
        send(*column(below_ref, half * cols, comps, line), 2 * (rows + 1) + half, comps, side)
        for r in range(rows):
            to = 2 * (r + 1) + half
            send(*column(pair, (2 * r + half) * cols, 3, lines), to, 3, side)
            send(*column(vec, (2 * r + half) * cols, rhs, lines), 3 * side + to, rhs, side)
    pairs = cols // 2
    for at in range(3 * rows):
        low = coef_ref[pl.ds(at * pairs * rhs, rhs), :]
        high = coef_ref[pl.ds((at * pairs + pairs - 1) * rhs, rhs), :]
        send(low, high, comps * side + at * rhs, rhs, 1)


def rows_kernel(rows, cols, rhs, leaf, later,
                mask_any, above_ref, below_ref, targets, factors, near_in,
                near_ref,
                near_mask, spread, values, sems):
    copies = start_all([(mask_any, near_mask)], sems)
    source_map = source_choice()
    for ref, line in ((above_ref, 0), (below_ref, 1)):
        for col in range(cols):
            place(ref, spread, values, source_map, rhs, col, cols, 2 * cols, line * cols + col)
    copies[0].wait()
    for at in range(rows * cols):
        row, col = at // cols, at % cols
        total = near_in[at]
        for slot in range(9):
            to_row, to_col = row + slot // 3 - 1, col + slot % 3 - 1
            if to_row >= rows and col < later:
                continue
            if not 0 <= to_row < rows and 0 <= to_col < cols:
                other = (0 if to_row < 0 else cols) + to_col
                total = total + tile_product(
                    spread[other], step_target(targets, factors, at, slot), values[other], near_mask[row, col, slot] != 0
                )
        near_ref[at] = total


def far_kernel(rows, cols, rhs, rank, far_list,
               far_any, left_ref, right_ref, coef_ref, coupling_any, basis_ref,
               far_ref,
               far_mask, coupling, dup, wide, sems):
    copies = start_all([(far_any, far_mask), (coupling_any, coupling)], sems)
    leaves = rows * cols
    low = lax.broadcasted_iota(jnp.int32, (rhs, 2 * rank), 1) < rank
    pairs = cols // 2
    for line in range(rows + 4):
        for pair in range(pairs + 2):
            if pair == 0:
                both = left_ref[pl.ds(line * rhs, rhs), :]
            elif pair == pairs + 1:
                both = right_ref[pl.ds(line * rhs, rhs), :]
            else:
                both = coef_ref[pl.ds((line * pairs + pair - 1) * rhs, rhs), :]
            turned = pltpu.roll(both, rank, 1)
            at = line * (cols + 4) + 2 * pair
            dup[at] = jnp.where(low, both, turned)
            dup[at + 1] = jnp.where(low, turned, both)
    copies[0].wait()
    for row in range(rows):
        for col in range(cols):
            at = row * cols + col
            for chunk in range(len(far_list) // 2):
                parts = []
                for slot in (2 * chunk, 2 * chunk + 1):
                    down_step, right_step = far_list[slot]
                    part = dup[(row + 2 + down_step) * (cols + 4) + col + 2 + right_step]
                    parts.append(jnp.where(far_mask[row, col, slot] != 0, part, 0.0))
                hi, lo = split(jnp.where(low, parts[0], parts[1]))
                wide[pl.ds(at * rhs, rhs), pl.ds(chunk * 2 * rank, 2 * rank)] = hi
                wide[pl.ds((leaves + at) * rhs, rhs), pl.ds(chunk * 2 * rank, 2 * rank)] = lo
    copies[1].wait()
    both = jnp.concatenate(split(jnp.concatenate([coupling[slot] for slot in range(len(far_list))], 1)), 0)
    four = dot(wide[...], both, NT)
    half = leaves * rhs
    far = (four[:half, :rank] + four[half:, :rank]) + (four[:half, rank:] + four[half:, rank:])
    for at in range(leaves):
        both = basis_ref[at]
        far_ref[at] = dot_parts(far[at * rhs : (at + 1) * rhs], both[:rank], both[rank:])


def side_kernel(rows, cols, rhs, leaf, later,
                mask_any, left_ref, right_ref, below_ref, targets, factors, near_ref, far_ref,
                base_ref,
                near_mask, spread, values, sems):
    copies = start_all([(mask_any, near_mask)], sems)
    source_map = source_choice()
    side = 2 * (rows + 2)
    for ref, first in ((left_ref, 0), (right_ref, rows + 2)):
        for line in range(rows + 2):
            place(ref, spread, values, source_map, rhs, 2 * line, 1, side, first + line)
    for col in range(later + 1):
        place(below_ref, spread, values, source_map, rhs, col, cols, 2 * cols, side + col)
    copies[0].wait()
    scale = 1.0 / (3.0 * float(leaf) ** 0.5)
    for at in range(rows * cols):
        row, col = at // cols, at % cols
        total = near_ref[at]
        for slot in range(9):
            to_row, to_col = row + slot // 3 - 1, col + slot % 3 - 1
            if not 0 <= to_col < cols:
                other = (0 if to_col < 0 else rows + 2) + to_row + 1
            elif to_row >= rows and col < later:
                other = side + to_col
            else:
                other = None
            if other is not None:
                total = total + tile_product(
                    spread[other], step_target(targets, factors, at, slot), values[other], near_mask[row, col, slot] != 0
                )
        base_ref[at] = total * scale + far_ref[at]


def finish_kernel(rows, cols, rhs, rank, nodes, owner_ref, top_ref, down_ref, base_ref, out_ref):
    lines = 2 * rows * cols
    high = (lax.broadcasted_iota(jnp.int32, (rhs, 2 * rank), 1) >= rank).astype(jnp.int32)
    owner = owner_ref[...] - high
    chosen = jnp.zeros((rhs, 2 * rank), F32)
    for pair in range(nodes // 2):
        chosen = jnp.where(owner == 2 * pair, top_ref[pl.ds(pair * rhs, rhs), :], chosen)
    local = (chosen + pltpu.roll(chosen, rank, 1))[:, :rank]
    for at in range(rows * cols):
        down = dot_parts(local, down_ref[at, pl.ds(0, rank)], down_ref[at, pl.ds(rank, rank)])
        start = (at // cols) * 2 * cols + at % cols
        put_strided(out_ref, start, cols, rhs, lines, base_ref[at] + down)


VMEM = pl.BlockSpec(memory_space=pltpu.VMEM)
SMEM = pl.BlockSpec(memory_space=pltpu.SMEM)
ANY = pl.BlockSpec(memory_space=pltpu.HBM)


def lanes(x):
    x = x.reshape(x.shape[:-1] + (2, 128))
    return jnp.swapaxes(x, -3, -2).reshape(-1, 128)


def on_device(
    vectors,
    leaf_order,
    offsets,
    near_mask,
    far_mask,
    basis,
    transfer,
    coupling,
    top_coupling,
    cluster_owner,
):
    rhs, rows, cols, leaf = vectors.shape
    rank = basis.shape[2]
    nodes = top_coupling.shape[0]
    leaves = rows * cols
    n_row, n_col = lax.axis_size("row"), lax.axis_size("col")
    devices = n_row * n_col
    col_even = lax.axis_index("col") % 2 == 0
    comps = 3 + rhs
    later = 3
    near_rows = comps * 2 * cols
    coef_rows = leaves // 2 * rhs
    top_rows = nodes // 2 * rhs
    halo_rows = near_rows + coef_rows

    def params():
        return pltpu.CompilerParams(vmem_limit_bytes=12 * 1024 * 1024)

    def grid_perm(step):
        return [
            (r * n_col + c, t[0] * n_col + t[1])
            for r in range(n_row)
            for c in range(n_col)
            for t in [step(r, c)]
            if t is not None
        ]

    def permute(x, step):
        return lax.ppermute(x, AXES, grid_perm(step))

    def sibling(r, c):
        return (r ^ 1, c)

    def odd_rows(r, c):
        t = r + 1 if r % 2 else r - 1
        return (t, c) if 0 <= t < n_row else None

    def other_row(r, c):
        return (n_row - 1 - r, c)

    def even_cols(r, c):
        return (r, c ^ 1)

    def odd_cols(r, c):
        t = c + 1 if c % 2 else c - 1
        return (r, t) if 0 <= t < n_col else None

    def doubled(x, step):
        return x + lax.ppermute(x, AXES, [(i, i ^ step) for i in range(devices)])

    def in_hbm(x):
        return pltpu.with_memory_space_constraint(x, pltpu.HBM)

    vec = lanes(vectors)
    transfer2 = transfer.reshape(leaves * rank, rank)
    pair, basis_own, sent, owner = pl.pallas_call(
        functools.partial(prepare_kernel, rows, cols, rhs, rank, leaf, nodes),
        out_shape=(
            jax.ShapeDtypeStruct((3 * 2 * leaves + coef_rows, 128), F32),
            jax.ShapeDtypeStruct((leaves, 2 * rank, leaf), BF16),
            jax.ShapeDtypeStruct((halo_rows + top_rows, 128), F32),
            jax.ShapeDtypeStruct((rhs, 2 * rank), jnp.int32),
        ),
        in_specs=[SMEM] + [ANY] * 6,
        out_specs=(VMEM,) * 4,
        scratch_shapes=[
            pltpu.VMEM((rhs * 2 * leaves, 128), F32),
            pltpu.VMEM((2 * leaves, 128), jnp.int32),
            pltpu.VMEM((3 * 2 * leaves, 128), F32),
            pltpu.VMEM((leaves, rank, leaf), F32),
            pltpu.VMEM((leaves * rank, rank), F32),
            pltpu.VMEM((nodes, rank, rank), F32),
            pltpu.VMEM((FEATS * 2 * leaves, 128), F32),
            pltpu.VMEM((nodes * rank, rank), F32),
            pltpu.SemaphoreType.DMA((6,)),
        ],
        compiler_params=params(),
        name="prepare",
    )(
        cluster_owner,
        in_hbm(vec),
        in_hbm(lanes(leaf_order)),
        in_hbm(lanes(offsets)),
        in_hbm(basis.reshape(leaves, rank, leaf)),
        in_hbm(transfer2),
        in_hbm(top_coupling),
    )

    top = sent[halo_rows:]
    merged = n_row == 4
    if merged:
        got = permute(sent, other_row)
    else:
        got = permute(sent[:halo_rows], odd_rows)
    pair_sib = permute(pair, sibling)
    vec_sib = permute(vec, sibling)

    near_slots = in_hbm(jnp.transpose(near_mask, (1, 2, 0)))
    far_slots = in_hbm(jnp.transpose(far_mask, (1, 2, 0)))
    near_table = pltpu.SMEM((rows, cols, 9), jnp.int32)
    near_shape = jax.ShapeDtypeStruct((leaves, rhs, leaf), F32)
    near, targets, factors = pl.pallas_call(
        functools.partial(own_kernel, rows, cols, rhs, rank, leaf),
        out_shape=(
            near_shape,
            jax.ShapeDtypeStruct((leaves, K, leaf), BF16),
            jax.ShapeDtypeStruct((9, K, 128), BF16),
        ),
        in_specs=[ANY, VMEM, VMEM],
        out_specs=(VMEM,) * 3,
        scratch_shapes=[
            near_table,
            pltpu.VMEM((FEATS * 2 * leaves, 128), F32),
            pltpu.VMEM((leaves, leaf, K), BF16),
            pltpu.VMEM((leaves, 2 * rhs, leaf), BF16),
            pltpu.SemaphoreType.DMA((1,)),
        ],
        compiler_params=params(),
        name="own",
    )(near_slots, vec, pair)

    got, near = lax.optimization_barrier((got, near))
    side_rows = comps * (rows + 2) * 2
    column_rows = side_rows + 3 * rows * rhs
    above, below, coef_mid, even_sent, odd_sent = pl.pallas_call(
        functools.partial(gather_kernel, rows, cols, rhs, n_row),
        out_shape=tuple(
            jax.ShapeDtypeStruct((count, 128), F32)
            for count in (near_rows, near_rows, 3 * coef_rows, column_rows + top_rows // 2, column_rows)
        ),
        in_specs=[ANY] * 4 + [VMEM],
        out_specs=(VMEM,) * 5,
        scratch_shapes=[
            pltpu.VMEM(vec.shape, F32),
            pltpu.VMEM(vec.shape, F32),
            pltpu.VMEM(pair.shape, F32),
            pltpu.VMEM(got.shape, F32),
            pltpu.SemaphoreType.DMA((4,)),
        ],
        compiler_params=params(),
        name="gather",
    )(vec, vec_sib, pair_sib, got, pair)

    if merged:
        top = top + got[halo_rows:]
    half = top_rows // 2
    row_even = lax.axis_index("row") % 2 == 0
    kept = permute(jnp.where(row_even, top[half:], top[:half]), sibling)
    top = jnp.where(row_even, top[:half], top[half:]) + kept
    even_sent = lax.dynamic_update_slice(even_sent, top, (column_rows, 0))
    got_even = permute(even_sent, even_cols)
    got_odd = permute(odd_sent, odd_cols)

    near = pl.pallas_call(
        functools.partial(rows_kernel, rows, cols, rhs, leaf, later),
        out_shape=near_shape,
        in_specs=[ANY] + [VMEM] * 5,
        out_specs=VMEM,
        scratch_shapes=[
            near_table,
            pltpu.VMEM((2 * cols, leaf, K), BF16),
            pltpu.VMEM((2 * cols, 2 * rhs, leaf), BF16),
            pltpu.SemaphoreType.DMA((1,)),
        ],
        compiler_params=params(),
        name="rows",
    )(near_slots, above, below, targets, factors, near)

    top, near = lax.optimization_barrier((top + got_even[column_rows:], near))
    left = jnp.where(col_even, got_odd, got_even[:column_rows])
    right = jnp.where(col_even, got_even[:column_rows], got_odd)

    steps = [] if merged else [n_col << k for k in range(1, n_row.bit_length() - 1)]
    steps += [2 << k for k in range(n_col.bit_length() - 2)]
    far = pl.pallas_call(
        functools.partial(far_kernel, rows, cols, rhs, rank, far_offsets()),
        out_shape=near_shape,
        in_specs=[ANY] + [VMEM] * 3 + [ANY, VMEM],
        out_specs=VMEM,
        scratch_shapes=[
            pltpu.SMEM((rows, cols, 16), jnp.int32),
            pltpu.VMEM(coupling.shape, F32),
            pltpu.VMEM(((rows + 4) * (cols + 4), rhs, 2 * rank), F32),
            pltpu.VMEM((2 * leaves * rhs, 16 * rank), BF16),
            pltpu.SemaphoreType.DMA((2,)),
        ],
        compiler_params=params(),
        name="far",
    )(far_slots, left[side_rows:], right[side_rows:], coef_mid, in_hbm(coupling), basis_own)

    top = doubled(top, steps[0])
    top, far, basis_own = lax.optimization_barrier((top, far, basis_own))
    down = pl.pallas_call(
        functools.partial(down_kernel, leaves, rank),
        out_shape=jax.ShapeDtypeStruct((leaves, 2 * rank, leaf), BF16),
        in_specs=[VMEM, VMEM],
        out_specs=VMEM,
        compiler_params=params(),
        name="down",
    )(basis_own, transfer2)

    for step in steps[1:]:
        top = doubled(top, step)

    sides = 2 * (rows + 2)
    base = pl.pallas_call(
        functools.partial(side_kernel, rows, cols, rhs, leaf, later),
        out_shape=near_shape,
        in_specs=[ANY] + [VMEM] * 7,
        out_specs=VMEM,
        scratch_shapes=[
            near_table,
            pltpu.VMEM((sides + later + 1, leaf, K), BF16),
            pltpu.VMEM((sides + later + 1, 2 * rhs, leaf), BF16),
            pltpu.SemaphoreType.DMA((1,)),
        ],
        compiler_params=params(),
        name="side",
    )(near_slots, left[:side_rows], right[:side_rows], below, targets, factors, near, far)

    top, base = lax.optimization_barrier((top, base))
    other = permute(top, sibling)
    other, down = lax.optimization_barrier((other, down))
    top = jnp.concatenate([jnp.where(row_even, top, other), jnp.where(row_even, other, top)], 0)
    out = pl.pallas_call(
        functools.partial(finish_kernel, rows, cols, rhs, rank, nodes),
        out_shape=jax.ShapeDtypeStruct((rhs * 2 * leaves, 128), F32),
        in_specs=[VMEM] * 4,
        out_specs=VMEM,
        compiler_params=params(),
        name="finish",
    )(owner, top, down, base)
    out = jnp.swapaxes(out.reshape(rhs, rows, 2, cols, 128), 2, 3)
    return out.reshape(rhs, rows, cols, leaf)


def solution(mesh):
    in_specs = (
        P(None, "row", "col", None),
        P("row", "col", None),
        P(None, "row", "col", None),
        P(None, "row", "col"),
        P(None, "row", "col"),
        P("row", "col", None, None),
        P("row", "col", None, None),
        P(),
        P(),
        P("row", "col"),
    )
    out_specs = P(None, "row", "col", None)
    return jax.shard_map(
        on_device, mesh=mesh, in_specs=in_specs, out_specs=out_specs, check_vma=False
    )
```

```python
import functools

import jax
import jax.numpy as jnp
import numpy as np
from jax import lax
from jax.experimental import pallas as pl
from jax.experimental.pallas import tpu as pltpu
from jax.sharding import PartitionSpec as P

softening = 0.01
F32 = jnp.float32
BF16 = jnp.bfloat16
AXES = ("row", "col")
NT = (((1,), (1,)), ((), ()))
TN = (((0,), (0,)), ((), ()))
NN = (((1,), (0,)), ((), ()))
FEATS = 16
K = 32


def far_offsets():
    found = []
    for down_step in range(-2, 3):
        for right_step in range(-2, 3):
            if max(abs(down_step), abs(right_step)) == 2:
                found.append((down_step, right_step))
    return found


def dot(a, b, dims=NN):
    return lax.dot_general(a, b, dims, preferred_element_type=F32)


def split(x):
    hi = x.astype(BF16)
    lo = (x - hi.astype(F32)).astype(BF16)
    return hi, lo


def dot_parts(a, b_hi, b_lo, dims=NN):
    rows = a.shape[0]
    both = jnp.concatenate(split(a), 0)
    first, second = dot(both, b_hi, dims), dot(both, b_lo, dims)
    return (first[:rows] + first[rows:]) + (second[:rows] + second[rows:])


def dot3(a, b, dims=NN):
    return dot_parts(a, *split(b), dims)


def strided(ref, start, half, count, stride):
    first = ref[pl.ds(start, count, stride=stride), :]
    second = ref[pl.ds(start + half, count, stride=stride), :]
    return jnp.concatenate([first, second], 1)


def put_strided(ref, start, half, count, stride, x):
    ref[pl.ds(start, count, stride=stride), :] = x[:, :128]
    ref[pl.ds(start + half, count, stride=stride), :] = x[:, 128:]


def products(slot):
    step = (slot // 3 - 1, slot % 3 - 1)
    one = 6
    found = []
    for comp in range(3):
        for mine in (comp, 8 + comp):
            for other in (comp, 8 + comp):
                found.append((mine, other, -2.0))
    for part in range(3):
        found.append((3 + part, one, 1.0))
        found.append((one, 3 + part, 1.0))
    for comp in range(2):
        for part in (comp, 8 + comp):
            found.append((part, one, 2.0 * step[comp]))
            found.append((one, part, -2.0 * step[comp]))
    rest = np.float32(softening)
    for _ in range(3):
        part = np.float32(np.asarray(rest, jnp.bfloat16))
        found.append((one, one, float(part)))
        rest = np.float32(rest - part)
    found.append((one, one, float(step[0] ** 2 + step[1] ** 2)))
    return found


def source_choice():
    feat = lax.broadcasted_iota(jnp.int32, (FEATS, K), 0)
    at = lax.broadcasted_iota(jnp.int32, (FEATS, K), 1)
    chosen = jnp.zeros((FEATS, K), F32)
    for i, (mine, _, _) in enumerate(products(0)):
        chosen = jnp.where((at == i) & (feat == mine), 1.0, chosen)
    return chosen.astype(BF16)


def target_choice():
    at = lax.broadcasted_iota(jnp.int32, (K, FEATS), 0)
    feat = lax.broadcasted_iota(jnp.int32, (K, FEATS), 1)
    chosen = jnp.zeros((K, FEATS), F32)
    for i, (_, other, _) in enumerate(products(0)):
        chosen = jnp.where((at == i) & (feat == other), 1.0, chosen)
    return chosen.astype(BF16)


def put_factors(factors):
    at = lax.broadcasted_iota(jnp.int32, (K, 128), 0)
    for slot in range(9):
        factor = jnp.zeros((K, 128), F32)
        for i, (_, _, value) in enumerate(products(slot)):
            if value:
                factor = jnp.where(at == i, value, factor)
        factors[slot] = factor.astype(BF16)


def start_all(pairs, sems):
    copies = [pltpu.make_async_copy(src, dst, sems.at[i]) for i, (src, dst) in enumerate(pairs)]
    for copy in copies:
        copy.start()
    return copies


def prepare_kernel(rows, cols, rhs, rank, leaf, nodes,
                   owner_ref, vec_any, order_any, off_any, basis_any, transfer_any, table_any,
                   pair_ref, basis_out, sent_ref, owner_out,
                   vec, order, off, basis, transfer, table, feat, rolled, sems):
    leaves = rows * cols
    lines = 2 * leaves
    copies = start_all(
        [(order_any, order), (off_any, off), (basis_any, basis), (vec_any, vec), (transfer_any, transfer), (table_any, table)],
        sems,
    )
    copies[0].wait()
    copies[1].wait()
    for comp in range(3):
        u = off[pl.ds(comp * lines, lines), :] - 0.5
        if comp == 2:
            u = u * 0.25
        hi = u.astype(BF16).astype(F32)
        feat[pl.ds(2 * comp * lines, lines), :] = hi
        feat[pl.ds((2 * comp + 1) * lines, lines), :] = (u - hi).astype(BF16).astype(F32)
    feat[pl.ds(6 * lines, 10 * lines), :] = jnp.zeros((10 * lines, 128), F32)
    copies[2].wait()
    copies[3].wait()
    spots = lax.broadcasted_iota(jnp.int32, (leaf, leaf), 0)
    offs = []
    for at in range(leaves):
        start = (at // cols) * 2 * cols + at % cols
        own_order = jnp.concatenate([order[pl.ds(start, 1), :], order[pl.ds(start + cols, 1), :]], 1)
        chosen = (jnp.broadcast_to(own_order, (leaf, leaf)) == spots).astype(F32).astype(BF16)
        bh, bl = split(basis[at])
        own = strided(feat, start, cols, FEATS, lines).astype(BF16)
        moved = dot(jnp.concatenate([bh, bl, own], 0), chosen, NT)
        basis_out[at] = moved[: 2 * rank].astype(BF16)
        offs.append(moved[2 * rank :])
    coefs = []
    for at in range(leaves):
        start = (at // cols) * 2 * cols + at % cols
        xh, xl = split(strided(vec, start, cols, rhs, lines))
        four = dot(jnp.concatenate([xh, xl], 0), basis_out[at], NT)
        coefs.append(four[:rhs, :rank] + four[:rhs, rank:] + four[rhs:, :rank] + four[rhs:, rank:])
    for at in range(leaves):
        start = (at // cols) * 2 * cols + at % cols
        for comp in range(3):
            line = offs[at][2 * comp : 2 * comp + 1] + offs[at][2 * comp + 1 : 2 * comp + 2]
            pair_ref[pl.ds(comp * lines + start, 1), :] = line[:, :128]
            pair_ref[pl.ds(comp * lines + start + cols, 1), :] = line[:, 128:]
    wide = [jnp.concatenate([coefs[2 * p], coefs[2 * p + 1]], 1) for p in range(leaves // 2)]
    row = jnp.where(lax.rem(lax.axis_index("row"), 2) == 0, 0, (rows - 1) * 2 * cols)
    for comp in range(3 + rhs):
        ref, first = (pair_ref, comp) if comp < 3 else (vec, comp - 3)
        sent_ref[pl.ds(comp * 2 * cols, 2 * cols), :] = ref[pl.ds(pl.multiple_of(first * lines + row, 2 * cols), 2 * cols), :]
    near_rows = (3 + rhs) * 2 * cols
    for p in range(leaves // 2):
        pair_ref[pl.ds(3 * lines + p * rhs, rhs), :] = wide[p]
        sent_ref[pl.ds(near_rows + p * rhs, rhs), :] = wide[p]
    copies[4].wait()
    cluster = dot3(jnp.concatenate(wide, 1), transfer[...])
    copies[5].wait()
    owner = owner_ref[0, 0]
    owner_out[...] = jnp.full(owner_out.shape, owner, jnp.int32)
    for node in range(nodes):
        gap = lax.rem(node - owner + nodes, nodes)
        rolled[pl.ds(node * rank, rank), :] = table[gap] * jnp.where(gap == 0, 0.0, 1.0)
    terms = dot3(cluster, rolled[...], NT)
    for pair in range(nodes // 2):
        sent_ref[pl.ds(near_rows + (leaves // 2 + pair) * rhs, rhs), :] = terms[:, pair * 2 * rank : (pair + 1) * 2 * rank]


def fill(into, ref, lines):
    total = jnp.zeros((lines, 128), F32)
    for comp in range(3):
        u = ref[pl.ds(comp * lines, lines), :]
        hi = u.astype(BF16).astype(F32)
        into[pl.ds(comp * lines, lines), :] = hi
        into[pl.ds((8 + comp) * lines, lines), :] = u - hi
        total = total + u * u
    for part in range(3):
        hi = total.astype(BF16).astype(F32)
        into[pl.ds((3 + part) * lines, lines), :] = hi
        total = total - hi
    into[pl.ds(6 * lines, lines), :] = jnp.ones((lines, 128), F32)
    for unused in (7, 11, 12, 13, 14, 15):
        into[pl.ds(unused * lines, lines), :] = jnp.zeros((lines, 128), F32)


def leaf_features(ref, start, half, stride):
    u = strided(ref, start, half, 8, stride)
    row = lax.broadcasted_iota(jnp.int32, u.shape, 0)
    u = jnp.where(row < 3, u, 0.0)
    hi = u.astype(BF16).astype(F32)
    first = hi
    total = jnp.sum(u * u, axis=0, keepdims=True)
    for part in range(3):
        square = total.astype(BF16).astype(F32)
        first = jnp.where(row == 3 + part, square, first)
        total = total - square
    first = jnp.where(row == 6, 1.0, first)
    return jnp.concatenate([first, u - hi], 0).astype(BF16)


def step_target(targets, factors, at, slot):
    factor = factors[slot]
    return targets[at] * jnp.concatenate([factor, factor], 1)


def place(points, spread, values, source_map, rhs, start, half, stride, at):
    spread[at] = dot(leaf_features(points, start, half, stride), source_map, TN).astype(BF16)
    xh, xl = split(strided(points, 3 * stride + start, half, rhs, stride))
    values[at] = jnp.concatenate([xh, xl], 0)


def tile_product(spread, target, values, keep):
    kh, kl = split(lax.rsqrt(dot(spread, target)))
    x = jnp.where(keep, values, jnp.zeros_like(values))
    rhs = x.shape[0] // 2
    first, second = dot(x, kh), dot(x, kl)
    return (first[:rhs] + first[rhs:]) + (second[:rhs] + second[rhs:])


def own_kernel(rows, cols, rhs, rank, leaf,
               mask_any, vec, pos_ref,
               near_ref, targets, factors,
               near_mask, feat, spread, values, sems):
    copies = start_all([(mask_any, near_mask)], sems)
    leaves = rows * cols
    lines = 2 * leaves
    fill(feat, pos_ref, lines)
    put_factors(factors)
    source_map, target_map = source_choice(), target_choice()
    for at in range(leaves):
        start = (at // cols) * 2 * cols + at % cols
        own = strided(feat, start, cols, FEATS, lines).astype(BF16)
        spread[at] = dot(own, source_map, TN).astype(BF16)
    for at in range(leaves):
        start = (at // cols) * 2 * cols + at % cols
        own = strided(feat, start, cols, FEATS, lines).astype(BF16)
        targets[at] = dot(target_map, own).astype(BF16)
    for at in range(leaves):
        start = (at // cols) * 2 * cols + at % cols
        xh, xl = split(strided(vec, start, cols, rhs, lines))
        values[at] = jnp.concatenate([xh, xl], 0)
    copies[0].wait()
    for at in range(leaves):
        row, col = at // cols, at % cols
        total = jnp.zeros((rhs, leaf), F32)
        for slot in range(9):
            to_row, to_col = row + slot // 3 - 1, col + slot % 3 - 1
            if 0 <= to_row < rows and 0 <= to_col < cols:
                other = to_row * cols + to_col
                total = total + tile_product(
                    spread[other], step_target(targets, factors, at, slot), values[other], near_mask[row, col, slot] != 0
                )
        near_ref[at] = total


def down_kernel(leaves, rank, basis_ref, transfer, down_ref):
    for at in range(leaves):
        both = basis_ref[at]
        th, tl = split(transfer[pl.ds(at * rank, rank), :])
        moved = dot(th, both[:rank], TN) + dot(tl, both[:rank], TN) + dot(th, both[rank:], TN)
        gh, gl = split(moved)
        down_ref[at] = jnp.concatenate([gh, gl], 0)


def gather_kernel(rows, cols, rhs, n_row,
                  vec_any, vec_sib_any, pair_sib_any, got_any, pair,
                  above_ref, below_ref, coef_ref, even_ref, odd_ref,
                  vec, vec_sib, pair_sib, got, sems):
    copies = start_all(
        [(vec_any, vec), (vec_sib_any, vec_sib), (pair_sib_any, pair_sib), (got_any, got)], sems
    )
    comps = 3 + rhs
    lines = 2 * rows * cols
    line = 2 * cols
    my_row = lax.axis_index("row")
    row_even = lax.rem(my_row, 2) == 0
    col_even = lax.rem(lax.axis_index("col"), 2) == 0
    beyond = jnp.where(row_even, my_row > 0, my_row < n_row - 1)
    for copy in copies:
        copy.wait()
    row = jnp.where(row_even, 0, (rows - 1) * line)
    for comp in range(comps):
        ref, first = (pair_sib, comp) if comp < 3 else (vec_sib, comp - 3)
        near = ref[pl.ds(pl.multiple_of(first * lines + row, line), line), :]
        mine = pl.ds(comp * line, line)
        far = jnp.where(beyond, got[mine, :], 0.0)
        above_ref[mine, :] = jnp.where(row_even, far, near)
        below_ref[mine, :] = jnp.where(row_even, near, far)
    block = rows * cols // 2 * rhs
    own_coef = pl.ds(3 * lines, block)
    near = pair_sib[own_coef, :]
    far = jnp.where(beyond, got[pl.ds(comps * line, block), :], 0.0)
    coef_ref[pl.ds(0, block), :] = jnp.where(row_even, far, near)
    coef_ref[pl.ds(block, block), :] = pair[own_coef, :]
    coef_ref[pl.ds(2 * block, block), :] = jnp.where(row_even, near, far)

    def send(low, high, start, count, stride):
        where = pl.ds(start, count) if stride == 1 else pl.ds(start, count, stride=stride)
        even_ref[where, :] = jnp.where(col_even, high, low)
        odd_ref[where, :] = jnp.where(col_even, low, high)

    def column(ref, start, count, stride):
        return [ref[pl.ds(start + at, count, stride=stride), :] for at in (0, cols - 1)]

    side = 2 * (rows + 2)
    for half in range(2):
        send(*column(above_ref, half * cols, comps, line), half, comps, side)
        send(*column(below_ref, half * cols, comps, line), 2 * (rows + 1) + half, comps, side)
        for r in range(rows):
            to = 2 * (r + 1) + half
            send(*column(pair, (2 * r + half) * cols, 3, lines), to, 3, side)
            send(*column(vec, (2 * r + half) * cols, rhs, lines), 3 * side + to, rhs, side)
    pairs = cols // 2
    for at in range(3 * rows):
        low = coef_ref[pl.ds(at * pairs * rhs, rhs), :]
        high = coef_ref[pl.ds((at * pairs + pairs - 1) * rhs, rhs), :]
        send(low, high, comps * side + at * rhs, rhs, 1)


def rows_kernel(rows, cols, rhs, leaf, later,
                mask_any, above_ref, below_ref, targets, factors, near_in,
                near_ref,
                near_mask, spread, values, sems):
    copies = start_all([(mask_any, near_mask)], sems)
    source_map = source_choice()
    for ref, line in ((above_ref, 0), (below_ref, 1)):
        for col in range(cols):
            place(ref, spread, values, source_map, rhs, col, cols, 2 * cols, line * cols + col)
    copies[0].wait()
    for at in range(rows * cols):
        row, col = at // cols, at % cols
        total = near_in[at]
        for slot in range(9):
            to_row, to_col = row + slot // 3 - 1, col + slot % 3 - 1
            if to_row >= rows and col < later:
                continue
            if not 0 <= to_row < rows and 0 <= to_col < cols:
                other = (0 if to_row < 0 else cols) + to_col
                total = total + tile_product(
                    spread[other], step_target(targets, factors, at, slot), values[other], near_mask[row, col, slot] != 0
                )
        near_ref[at] = total


def far_kernel(rows, cols, rhs, rank, far_list,
               far_any, left_ref, right_ref, coef_ref, coupling_any, basis_ref,
               far_ref,
               far_mask, coupling, dup, wide, sems):
    copies = start_all([(far_any, far_mask), (coupling_any, coupling)], sems)
    leaves = rows * cols
    low = lax.broadcasted_iota(jnp.int32, (rhs, 2 * rank), 1) < rank
    pairs = cols // 2
    for line in range(rows + 4):
        for pair in range(pairs + 2):
            if pair == 0:
                both = left_ref[pl.ds(line * rhs, rhs), :]
            elif pair == pairs + 1:
                both = right_ref[pl.ds(line * rhs, rhs), :]
            else:
                both = coef_ref[pl.ds((line * pairs + pair - 1) * rhs, rhs), :]
            turned = pltpu.roll(both, rank, 1)
            at = line * (cols + 4) + 2 * pair
            dup[at] = jnp.where(low, both, turned)
            dup[at + 1] = jnp.where(low, turned, both)
    copies[0].wait()
    for row in range(rows):
        for col in range(cols):
            at = row * cols + col
            for chunk in range(len(far_list) // 2):
                parts = []
                for slot in (2 * chunk, 2 * chunk + 1):
                    down_step, right_step = far_list[slot]
                    part = dup[(row + 2 + down_step) * (cols + 4) + col + 2 + right_step]
                    parts.append(jnp.where(far_mask[row, col, slot] != 0, part, 0.0))
                hi, lo = split(jnp.where(low, parts[0], parts[1]))
                wide[pl.ds(at * rhs, rhs), pl.ds(chunk * 2 * rank, 2 * rank)] = hi
                wide[pl.ds((leaves + at) * rhs, rhs), pl.ds(chunk * 2 * rank, 2 * rank)] = lo
    copies[1].wait()
    both = jnp.concatenate(split(jnp.concatenate([coupling[slot] for slot in range(len(far_list))], 1)), 0)
    four = dot(wide[...], both, NT)
    half = leaves * rhs
    far = (four[:half, :rank] + four[half:, :rank]) + (four[:half, rank:] + four[half:, rank:])
    for at in range(leaves):
        both = basis_ref[at]
        far_ref[at] = dot_parts(far[at * rhs : (at + 1) * rhs], both[:rank], both[rank:])


def side_kernel(rows, cols, rhs, leaf, later,
                mask_any, left_ref, right_ref, below_ref, targets, factors, near_ref, far_ref,
                base_ref,
                near_mask, spread, values, sems):
    copies = start_all([(mask_any, near_mask)], sems)
    source_map = source_choice()
    side = 2 * (rows + 2)
    for ref, first in ((left_ref, 0), (right_ref, rows + 2)):
        for line in range(rows + 2):
            place(ref, spread, values, source_map, rhs, 2 * line, 1, side, first + line)
    for col in range(later + 1):
        place(below_ref, spread, values, source_map, rhs, col, cols, 2 * cols, side + col)
    copies[0].wait()
    scale = 1.0 / (3.0 * float(leaf) ** 0.5)
    for at in range(rows * cols):
        row, col = at // cols, at % cols
        total = near_ref[at]
        for slot in range(9):
            to_row, to_col = row + slot // 3 - 1, col + slot % 3 - 1
            if not 0 <= to_col < cols:
                other = (0 if to_col < 0 else rows + 2) + to_row + 1
            elif to_row >= rows and col < later:
                other = side + to_col
            else:
                other = None
            if other is not None:
                total = total + tile_product(
                    spread[other], step_target(targets, factors, at, slot), values[other], near_mask[row, col, slot] != 0
                )
        base_ref[at] = total * scale + far_ref[at]


def finish_kernel(rows, cols, rhs, rank, nodes, owner_ref, top_ref, down_ref, base_ref, out_ref):
    lines = 2 * rows * cols
    high = (lax.broadcasted_iota(jnp.int32, (rhs, 2 * rank), 1) >= rank).astype(jnp.int32)
    owner = owner_ref[...] - high
    chosen = jnp.zeros((rhs, 2 * rank), F32)
    for pair in range(nodes // 2):
        chosen = jnp.where(owner == 2 * pair, top_ref[pl.ds(pair * rhs, rhs), :], chosen)
    local = (chosen + pltpu.roll(chosen, rank, 1))[:, :rank]
    for at in range(rows * cols):
        down = dot_parts(local, down_ref[at, pl.ds(0, rank)], down_ref[at, pl.ds(rank, rank)])
        start = (at // cols) * 2 * cols + at % cols
        put_strided(out_ref, start, cols, rhs, lines, base_ref[at] + down)


VMEM = pl.BlockSpec(memory_space=pltpu.VMEM)
SMEM = pl.BlockSpec(memory_space=pltpu.SMEM)
ANY = pl.BlockSpec(memory_space=pltpu.HBM)


def lanes(x):
    x = x.reshape(x.shape[:-1] + (2, 128))
    return jnp.swapaxes(x, -3, -2).reshape(-1, 128)


def on_device(
    vectors,
    leaf_order,
    offsets,
    near_mask,
    far_mask,
    basis,
    transfer,
    coupling,
    top_coupling,
    cluster_owner,
):
    rhs, rows, cols, leaf = vectors.shape
    rank = basis.shape[2]
    nodes = top_coupling.shape[0]
    leaves = rows * cols
    n_row, n_col = lax.axis_size("row"), lax.axis_size("col")
    devices = n_row * n_col
    col_even = lax.axis_index("col") % 2 == 0
    comps = 3 + rhs
    later = 4
    near_rows = comps * 2 * cols
    coef_rows = leaves // 2 * rhs
    top_rows = nodes // 2 * rhs
    halo_rows = near_rows + coef_rows

    def params():
        return pltpu.CompilerParams(vmem_limit_bytes=12 * 1024 * 1024)

    def grid_perm(step):
        return [
            (r * n_col + c, t[0] * n_col + t[1])
            for r in range(n_row)
            for c in range(n_col)
            for t in [step(r, c)]
            if t is not None
        ]

    def permute(x, step):
        return lax.ppermute(x, AXES, grid_perm(step))

    def sibling(r, c):
        return (r ^ 1, c)

    def odd_rows(r, c):
        t = r + 1 if r % 2 else r - 1
        return (t, c) if 0 <= t < n_row else None

    def other_row(r, c):
        return (n_row - 1 - r, c)

    def even_cols(r, c):
        return (r, c ^ 1)

    def odd_cols(r, c):
        t = c + 1 if c % 2 else c - 1
        return (r, t) if 0 <= t < n_col else None

    def doubled(x, step):
        return x + lax.ppermute(x, AXES, [(i, i ^ step) for i in range(devices)])

    def in_hbm(x):
        return pltpu.with_memory_space_constraint(x, pltpu.HBM)

    vec = lanes(vectors)
    transfer2 = transfer.reshape(leaves * rank, rank)
    pair, basis_own, sent, owner = pl.pallas_call(
        functools.partial(prepare_kernel, rows, cols, rhs, rank, leaf, nodes),
        out_shape=(
            jax.ShapeDtypeStruct((3 * 2 * leaves + coef_rows, 128), F32),
            jax.ShapeDtypeStruct((leaves, 2 * rank, leaf), BF16),
            jax.ShapeDtypeStruct((halo_rows + top_rows, 128), F32),
            jax.ShapeDtypeStruct((rhs, 2 * rank), jnp.int32),
        ),
        in_specs=[SMEM] + [ANY] * 6,
        out_specs=(VMEM,) * 4,
        scratch_shapes=[
            pltpu.VMEM((rhs * 2 * leaves, 128), F32),
            pltpu.VMEM((2 * leaves, 128), jnp.int32),
            pltpu.VMEM((3 * 2 * leaves, 128), F32),
            pltpu.VMEM((leaves, rank, leaf), F32),
            pltpu.VMEM((leaves * rank, rank), F32),
            pltpu.VMEM((nodes, rank, rank), F32),
            pltpu.VMEM((FEATS * 2 * leaves, 128), F32),
            pltpu.VMEM((nodes * rank, rank), F32),
            pltpu.SemaphoreType.DMA((6,)),
        ],
        compiler_params=params(),
        name="prepare",
    )(
        cluster_owner,
        in_hbm(vec),
        in_hbm(lanes(leaf_order)),
        in_hbm(lanes(offsets)),
        in_hbm(basis.reshape(leaves, rank, leaf)),
        in_hbm(transfer2),
        in_hbm(top_coupling),
    )

    top = sent[halo_rows:]
    merged = n_row == 4
    if merged:
        got = permute(sent, other_row)
    else:
        got = permute(sent[:halo_rows], odd_rows)
    pair_sib = permute(pair, sibling)
    vec_sib = permute(vec, sibling)

    near_slots = in_hbm(jnp.transpose(near_mask, (1, 2, 0)))
    far_slots = in_hbm(jnp.transpose(far_mask, (1, 2, 0)))
    near_table = pltpu.SMEM((rows, cols, 9), jnp.int32)
    near_shape = jax.ShapeDtypeStruct((leaves, rhs, leaf), F32)
    near, targets, factors = pl.pallas_call(
        functools.partial(own_kernel, rows, cols, rhs, rank, leaf),
        out_shape=(
            near_shape,
            jax.ShapeDtypeStruct((leaves, K, leaf), BF16),
            jax.ShapeDtypeStruct((9, K, 128), BF16),
        ),
        in_specs=[ANY, VMEM, VMEM],
        out_specs=(VMEM,) * 3,
        scratch_shapes=[
            near_table,
            pltpu.VMEM((FEATS * 2 * leaves, 128), F32),
            pltpu.VMEM((leaves, leaf, K), BF16),
            pltpu.VMEM((leaves, 2 * rhs, leaf), BF16),
            pltpu.SemaphoreType.DMA((1,)),
        ],
        compiler_params=params(),
        name="own",
    )(near_slots, vec, pair)

    got, near = lax.optimization_barrier((got, near))
    side_rows = comps * (rows + 2) * 2
    column_rows = side_rows + 3 * rows * rhs
    above, below, coef_mid, even_sent, odd_sent = pl.pallas_call(
        functools.partial(gather_kernel, rows, cols, rhs, n_row),
        out_shape=tuple(
            jax.ShapeDtypeStruct((count, 128), F32)
            for count in (near_rows, near_rows, 3 * coef_rows, column_rows + top_rows // 2, column_rows)
        ),
        in_specs=[ANY] * 4 + [VMEM],
        out_specs=(VMEM,) * 5,
        scratch_shapes=[
            pltpu.VMEM(vec.shape, F32),
            pltpu.VMEM(vec.shape, F32),
            pltpu.VMEM(pair.shape, F32),
            pltpu.VMEM(got.shape, F32),
            pltpu.SemaphoreType.DMA((4,)),
        ],
        compiler_params=params(),
        name="gather",
    )(vec, vec_sib, pair_sib, got, pair)

    if merged:
        top = top + got[halo_rows:]
    half = top_rows // 2
    row_even = lax.axis_index("row") % 2 == 0
    kept = permute(jnp.where(row_even, top[half:], top[:half]), sibling)
    top = jnp.where(row_even, top[:half], top[half:]) + kept
    even_sent = lax.dynamic_update_slice(even_sent, top, (column_rows, 0))
    got_even = permute(even_sent, even_cols)
    got_odd = permute(odd_sent, odd_cols)

    near = pl.pallas_call(
        functools.partial(rows_kernel, rows, cols, rhs, leaf, later),
        out_shape=near_shape,
        in_specs=[ANY] + [VMEM] * 5,
        out_specs=VMEM,
        scratch_shapes=[
            near_table,
            pltpu.VMEM((2 * cols, leaf, K), BF16),
            pltpu.VMEM((2 * cols, 2 * rhs, leaf), BF16),
            pltpu.SemaphoreType.DMA((1,)),
        ],
        compiler_params=params(),
        name="rows",
    )(near_slots, above, below, targets, factors, near)

    top, near = lax.optimization_barrier((top + got_even[column_rows:], near))
    left = jnp.where(col_even, got_odd, got_even[:column_rows])
    right = jnp.where(col_even, got_even[:column_rows], got_odd)

    steps = [] if merged else [n_col << k for k in range(1, n_row.bit_length() - 1)]
    steps += [2 << k for k in range(n_col.bit_length() - 2)]
    far = pl.pallas_call(
        functools.partial(far_kernel, rows, cols, rhs, rank, far_offsets()),
        out_shape=near_shape,
        in_specs=[ANY] + [VMEM] * 3 + [ANY, VMEM],
        out_specs=VMEM,
        scratch_shapes=[
            pltpu.SMEM((rows, cols, 16), jnp.int32),
            pltpu.VMEM(coupling.shape, F32),
            pltpu.VMEM(((rows + 4) * (cols + 4), rhs, 2 * rank), F32),
            pltpu.VMEM((2 * leaves * rhs, 16 * rank), BF16),
            pltpu.SemaphoreType.DMA((2,)),
        ],
        compiler_params=params(),
        name="far",
    )(far_slots, left[side_rows:], right[side_rows:], coef_mid, in_hbm(coupling), basis_own)

    top = doubled(top, steps[0])
    top, far, basis_own = lax.optimization_barrier((top, far, basis_own))
    down = pl.pallas_call(
        functools.partial(down_kernel, leaves, rank),
        out_shape=jax.ShapeDtypeStruct((leaves, 2 * rank, leaf), BF16),
        in_specs=[VMEM, VMEM],
        out_specs=VMEM,
        compiler_params=params(),
        name="down",
    )(basis_own, transfer2)

    for step in steps[1:]:
        top = doubled(top, step)

    sides = 2 * (rows + 2)
    base = pl.pallas_call(
        functools.partial(side_kernel, rows, cols, rhs, leaf, later),
        out_shape=near_shape,
        in_specs=[ANY] + [VMEM] * 7,
        out_specs=VMEM,
        scratch_shapes=[
            near_table,
            pltpu.VMEM((sides + later + 1, leaf, K), BF16),
            pltpu.VMEM((sides + later + 1, 2 * rhs, leaf), BF16),
            pltpu.SemaphoreType.DMA((1,)),
        ],
        compiler_params=params(),
        name="side",
    )(near_slots, left[:side_rows], right[:side_rows], below, targets, factors, near, far)

    top, base = lax.optimization_barrier((top, base))
    other = permute(top, sibling)
    other, down = lax.optimization_barrier((other, down))
    top = jnp.concatenate([jnp.where(row_even, top, other), jnp.where(row_even, other, top)], 0)
    out = pl.pallas_call(
        functools.partial(finish_kernel, rows, cols, rhs, rank, nodes),
        out_shape=jax.ShapeDtypeStruct((rhs * 2 * leaves, 128), F32),
        in_specs=[VMEM] * 4,
        out_specs=VMEM,
        compiler_params=params(),
        name="finish",
    )(owner, top, down, base)
    out = jnp.swapaxes(out.reshape(rhs, rows, 2, cols, 128), 2, 3)
    return out.reshape(rhs, rows, cols, leaf)


def solution(mesh):
    in_specs = (
        P(None, "row", "col", None),
        P("row", "col", None),
        P(None, "row", "col", None),
        P(None, "row", "col"),
        P(None, "row", "col"),
        P("row", "col", None, None),
        P("row", "col", None, None),
        P(),
        P(),
        P("row", "col"),
    )
    out_specs = P(None, "row", "col", None)
    return jax.shard_map(
        on_device, mesh=mesh, in_specs=in_specs, out_specs=out_specs, check_vma=False
    )
```
